256 devices in a mesh: seq: 64 (over y_lo, x, z), batch: 4 (over y_hi, core).
Axes of the slice: x: 4, y: 4 (y_hi: 2, y_lo: 2; y = y_hi * 2 + y_lo), z: 8, core: 2. Of those that a mesh axis runs over, the one named last changes fastest.
Arguments:
- tokens: bfloat16 [131072, 1024], P(('batch', 'seq')), parts along dimension 0, may hold values from -22 to 120.5
- router: bfloat16 [64, 1024], P('seq'), may hold values from -3 to 3
- w_in: bfloat16 [64, 1024, 2048], P('seq'), may hold values from -0.1875 to 0.1875
- w_out: bfloat16 [64, 2048, 1024], P('seq'), may hold values from -0.125 to 0.125
- cotangent: bfloat16 [131072, 1024], P(('batch', 'seq')), parts along dimension 0, may hold values from -6 to 6
Outputs:
- mixed: bfloat16 [131072, 1024], P(('batch', 'seq')), parts along dimension 0
- grad_tokens: bfloat16 [131072, 1024], P(('batch', 'seq')), parts along dimension 0
- grad_router: float32 [256, 1024], P(('batch', 'seq')), parts along dimension 0
The draws below stay inside these ranges and needn't reach their ends.
There are 4 independent parts, one for each index of `batch`. The reference program is written for one: setup_inputs(seed, part) draws one part's arguments, and reference() takes and returns one part's arrays. A program takes and returns all parts, laid end to end along the dimension named above; an argument that names none is the same for every part. Nothing has to cross between parts.
All inputs are finite; a program needn't handle non-finite values.
Results may differ from the reference program's by a relative error of at most 0.022.
Values may be sent and summed in bfloat16 or wider, within the bound.
A program may use at most 64 MiB of HBM per device.

```python
import math
import jax
import jax.numpy as jnp
from jax import lax

D = 1024
H = 2048
EXPERTS = 64
TOKENS = 32768


def draw_tokens(key, part):
    key = jax.random.fold_in(key, 7)
    key_base = jax.random.fold_in(key, 0)
    key_common = jax.random.fold_in(key, 2)
    key_phase = jax.random.fold_in(key, 3)
    index = jnp.arange(TOKENS)
    rise = 0.7 + 1.4 * index.astype(jnp.float32) / max(TOKENS - 1, 1)
    noise = jnp.clip(jax.random.normal(key_base, (TOKENS, D), jnp.float32), -6.0, 6.0) * rise[:, None]
    common = jnp.clip(jax.random.normal(key_common, (D,), jnp.float32), -3.0, 3.0) * 2.0
    phase = jax.random.uniform(key_phase, (), jnp.float32, 0.0, 2.0 * math.pi)
    place = index.astype(jnp.float32) / TOKENS
    drift = 1.0 + 0.5 * jnp.sin(2.0 * math.pi * 3.0 * place + phase)
    base = noise + drift[:, None] * common[None, :]
    return base.astype(jnp.bfloat16)


def draw_router(key, part):
    key = jax.random.fold_in(key, 19)
    spread = 0.4 / math.sqrt(D)
    noise = jnp.clip(jax.random.normal(key, (EXPERTS, D), jnp.float32), -6.0, 6.0) * spread
    return noise.astype(jnp.bfloat16)


def level_of(own_key, shape, cuts, least, high):
    gain, own = 1.0, jax.random.fold_in(own_key, 6)
    for position, parts in cuts:
        draws = jnp.exp(jax.random.uniform(jax.random.fold_in(own, position), (parts,), jnp.float32, least / len(cuts), high / len(cuts)))
        gain = gain * jnp.repeat(draws, shape[position] // parts).reshape([-1 if axis == position else 1 for axis in range(len(shape))])
    return gain


def normal_values(stream_key, extent, scale, bound, cuts=(), dtype=jnp.bfloat16):
    entries = jax.random.normal(stream_key, extent, jnp.float32) * scale
    if len(cuts) > 0:
        entries = level_of(stream_key, extent, cuts, -0.22, 0.18) * entries
    return jnp.clip(entries, min=-bound, max=bound).astype(dtype)


def setup_inputs(seed: int = 0, part: int = 0) -> dict:
    arg_keys = jax.random.split(jax.random.key(seed), 6)
    part_splits = jax.random.split(jax.random.fold_in(arg_keys[5], part), 6)
    return {
        "tokens": draw_tokens(jax.random.fold_in(jax.random.fold_in(arg_keys[5], part), 71), part),
        "router": draw_router(jax.random.fold_in(arg_keys[5], 71), part),
        "w_in": normal_values(arg_keys[2], (EXPERTS, D, H), D ** -0.5, 0.1875, ((0, 64),)),
        "w_out": normal_values(arg_keys[3], (EXPERTS, H, D), H ** -0.5, 0.125, ((0, 64),)),
        "cotangent": normal_values(part_splits[4], (TOKENS, D), 1.0, 6.0, ((0, 64),)),
    }


GELU_C = 0.7978845608028654
GELU_K = 0.044715


def gelu_parts(pre_act):
    inner = GELU_C * (pre_act + GELU_K * pre_act * pre_act * pre_act)
    tanh_v = jnp.tanh(inner)
    gelu_value = 0.5 * pre_act * (1.0 + tanh_v)
    gelu_slope = 0.5 * (1.0 + tanh_v) + 0.5 * pre_act * (1.0 - tanh_v * tanh_v) * GELU_C * (1.0 + 3.0 * GELU_K * pre_act * pre_act)
    return gelu_value, gelu_slope


def reference(tokens, router, w_in, w_out, cotangent):
    logits = jnp.dot(tokens, router.T, preferred_element_type=jnp.float32)
    col_peak = jnp.max(logits, axis=0, keepdims=True)
    exp_terms = jnp.exp(logits - col_peak)
    dispatch = exp_terms / jnp.sum(exp_terms, axis=0, keepdims=True)
    dispatch_b = dispatch.astype(jnp.bfloat16)
    combine = jax.nn.softmax(logits, axis=1)
    combine_b = combine.astype(jnp.bfloat16)
    slot_b = jnp.dot(dispatch_b.T, tokens, preferred_element_type=jnp.float32).astype(jnp.bfloat16)
    pre_act = lax.map(lambda pair: jnp.dot(pair[0][None, :], pair[1], preferred_element_type=jnp.float32)[0], (slot_b, w_in))
    gelu_value, gelu_slope = gelu_parts(pre_act)
    hidden_b = gelu_value.astype(jnp.bfloat16)
    slot_out = lax.map(lambda pair: jnp.dot(pair[0][None, :], pair[1], preferred_element_type=jnp.float32)[0], (hidden_b, w_out)).astype(jnp.bfloat16)
    mixed = jnp.dot(combine_b, slot_out, preferred_element_type=jnp.float32).astype(jnp.bfloat16)
    grad_comb = jnp.dot(cotangent, slot_out.T, preferred_element_type=jnp.float32)
    comb_inner = jnp.sum(combine * grad_comb, axis=1, keepdims=True)
    logit_comb = (combine * (grad_comb - comb_inner)).astype(jnp.bfloat16)
    grad_out = jnp.dot(combine_b.T, cotangent, preferred_element_type=jnp.float32).astype(jnp.bfloat16)
    grad_hidden = lax.map(lambda pair: jnp.dot(pair[1], pair[0][:, None], preferred_element_type=jnp.float32)[:, 0], (grad_out, w_out))
    grad_pre = (grad_hidden * gelu_slope).astype(jnp.bfloat16)
    grad_in = lax.map(lambda pair: jnp.dot(pair[1], pair[0][:, None], preferred_element_type=jnp.float32)[:, 0], (grad_pre, w_in)).astype(jnp.bfloat16)
    grad_disp = jnp.dot(tokens, grad_in.T, preferred_element_type=jnp.float32)
    disp_inner = jnp.sum(dispatch * grad_disp, axis=0, keepdims=True)
    logit_disp = (dispatch * (grad_disp - disp_inner)).astype(jnp.bfloat16)
    grad_tokens = (jnp.dot(dispatch_b, grad_in, preferred_element_type=jnp.float32)
                   + jnp.dot(logit_comb, router, preferred_element_type=jnp.float32)
                   + jnp.dot(logit_disp, router, preferred_element_type=jnp.float32)).astype(jnp.bfloat16)
    grad_router = (jnp.dot(logit_comb.T, tokens, preferred_element_type=jnp.float32)
                   + jnp.dot(logit_disp.T, tokens, preferred_element_type=jnp.float32))
    return mixed, grad_tokens, grad_router
```

```python
import functools

import jax
import jax.numpy as jnp
from jax import lax
from jax.experimental import pallas as pl
from jax.experimental.pallas import tpu as pltpu
from jax.sharding import PartitionSpec as P

GELU_C = 0.7978845608028654
GELU_K = 0.044715
MESH = pl.DeviceIdType.MESH
F32, BF16 = jnp.float32, jnp.bfloat16

GROUPS, PLACES = 8, 8
SLOTS = GROUPS * PLACES
TOK = 512
D = 1024
H = 2048
ROWS = D // 128
WIDE = 2 * D + 128
PACK = 2 * ROWS + 8


def gelu_parts(pre_act):
    inner = GELU_C * (pre_act + GELU_K * pre_act * pre_act * pre_act)
    tanh_v = jnp.tanh(inner)
    gelu_value = 0.5 * pre_act * (1.0 + tanh_v)
    gelu_slope = 0.5 * (1.0 + tanh_v) + 0.5 * pre_act * (1.0 - tanh_v * tanh_v) * GELU_C * (
        1.0 + 3.0 * GELU_K * pre_act * pre_act
    )
    return (gelu_value, gelu_slope)


def dot(left, right):
    return jnp.dot(left, right, preferred_element_type=F32)


def tail_dot(left, right):
    return lax.dot_general(left, right, (((1,), (1,)), ((), ())), preferred_element_type=F32)


def lead_dot(left, right):
    return lax.dot_general(left, right, (((0,), (0,)), ((), ())), preferred_element_type=F32)


def as_row(ref, first):
    return jnp.concatenate([ref[first + j : first + j + 1, :] for j in range(ROWS)], axis=1)


def kernel(
    tok_h, router_ref, win_h, wout_h, cot_h,
    mixed_ref, gtok_ref, grout_ref,
    tok, cot, win, wout, own, keys, key_in,
    ex_s, comb_s, combb_s, part, land1, pack, land2, packed, rows_s,
    sg, sg_f, stat, stat_own, out_b, back, land3, back2, land4, coef,
    load_sem, send_sem, recv_sem,
):
    me = lax.axis_index("seq")
    group, place = me // PLACES, lax.rem(me, PLACES)

    loads = [
        pltpu.make_async_copy(src, dst, load_sem.at[i])
        for i, (src, dst) in enumerate(
            ((tok_h, tok), (cot_h, cot), (win_h.at[0], win), (wout_h.at[0], wout))
        )
    ]
    for load in loads:
        load.start()

    def place_peer(k):
        p = lax.rem(place + k, PLACES)
        return p, {"seq": group * PLACES + p}

    def group_peer(k):
        g = lax.rem(group + k, GROUPS)
        return g, {"seq": g * PLACES + place}

    barrier = pltpu.get_barrier_semaphore()
    for k in range(1, 8):
        pl.semaphore_signal(barrier, inc=1, device_id=place_peer(k)[1], device_id_type=MESH)
        pl.semaphore_signal(barrier, inc=1, device_id=group_peer(k)[1], device_id_type=MESH)

    def send(stage, peer_of, src_of, dst):
        for k in range(1, 8):
            p, peer = peer_of(k)
            pltpu.make_async_remote_copy(
                src_ref=src_of(p), dst_ref=dst,
                send_sem=send_sem.at[stage], recv_sem=recv_sem.at[stage],
                device_id=peer, device_id_type=MESH,
            ).start()

    def landed(stage, seven):
        pltpu.make_async_copy(seven, seven, recv_sem.at[stage]).wait()

    def sent(stage, seven):
        pltpu.make_async_copy(seven, seven, send_sem.at[stage]).wait()

    def eight(first):
        return pl.ds(pl.multiple_of(first * 8, 8), 8)

    key_row = router_ref[...].astype(F32)
    for j in range(ROWS):
        own[j : j + 1, :] = key_row[:, 128 * j : 128 * (j + 1)]
    keys[eight(me), :] = own[...]
    pack[...] = jnp.zeros_like(pack)
    pl.semaphore_wait(barrier, 14)
    send(0, place_peer, lambda p: keys.at[eight(me)], keys.at[eight(me)])
    landed(0, keys.at[pl.ds(0, 56)])
    block = pl.ds(pl.multiple_of(group * 64, 64), 64)
    send(1, group_peer, lambda p: keys.at[block], keys.at[block])
    landed(1, keys.at[pl.ds(0, 448)])
    for j in range(ROWS):
        key_in[SLOTS:, 128 * j : 128 * (j + 1)] = keys[pl.ds(j, SLOTS, stride=8), :].astype(BF16)

    loads[0].wait()
    logit_t = tail_dot(key_in[SLOTS:, :], tok[...])
    peak = jnp.max(logit_t, axis=1, keepdims=True)
    ex = jnp.exp(logit_t - peak)
    ex_s[...] = ex
    ex_b = ex.astype(BF16)
    total = jnp.sum(ex, axis=1, keepdims=True)
    total_b = jnp.sum(ex_b.astype(F32), axis=1, keepdims=True)
    lane = lax.broadcasted_iota(jnp.int32, (SLOTS, 128), 1)
    part[:, 2 * D :] = jnp.where(lane == 0, peak, jnp.where(lane == 1, total, total_b))
    part[:, :D] = dot(ex_b, tok[...])
    row_peak = jnp.max(logit_t, axis=0, keepdims=True)
    row_ex = jnp.exp(logit_t - row_peak)
    comb = row_ex / jnp.sum(row_ex, axis=0, keepdims=True)
    comb_s[...] = comb
    combb_s[...] = comb.astype(BF16)
    loads[1].wait()
    part[:, D : 2 * D] = dot(combb_s[...], cot[...])

    send(2, group_peer, lambda g: part.at[eight(g)], land1.at[group])
    land1[group] = part[eight(group), :]
    landed(2, land1.at[pl.ds(0, 7)])
    peaks = land1[:, :, 2 * D : 2 * D + 1]
    high = jnp.max(peaks, axis=0, keepdims=True)
    scale = jnp.exp(peaks - high)
    slot_sum = jnp.sum(land1[:, :, :D] * scale, axis=0)
    gout_sum = jnp.sum(land1[:, :, D : 2 * D], axis=0)
    stat_sum = jnp.sum(land1[:, :, 2 * D :] * scale, axis=0)
    lane = lax.broadcasted_iota(jnp.int32, (8, 128), 1)
    stat_sum = jnp.where(lane == 0, high[0], stat_sum)
    for j in range(ROWS):
        pack[pl.ds(j, 8, stride=PACK), :] = slot_sum[:, 128 * j : 128 * (j + 1)]
        pack[pl.ds(ROWS + j, 8, stride=PACK), :] = gout_sum[:, 128 * j : 128 * (j + 1)]
    pack[pl.ds(2 * ROWS, 8, stride=PACK), :] = stat_sum

    def packed_of(p):
        return pl.ds(pl.multiple_of(p * PACK, 8), PACK)

    send(3, place_peer, lambda p: pack.at[packed_of(p)], land2.at[place])
    land2[place] = pack[packed_of(place), :]
    landed(3, land2.at[pl.ds(0, 7)])
    peaks = land2[:, 2 * ROWS : 2 * ROWS + 1, 0:1]
    high = jnp.max(peaks, axis=0, keepdims=True)
    scale = jnp.exp(peaks - high)
    stat_sum = jnp.sum(land2[:, 2 * ROWS : 2 * ROWS + 1, :] * scale, axis=0)
    slot_in = jnp.sum(land2[:, :ROWS, :] * scale, axis=0) / stat_sum[:, 2:3]
    packed[:ROWS, :] = slot_in
    packed[ROWS:, :] = jnp.sum(land2[:, ROWS : 2 * ROWS, :], axis=0)

    slot_row = as_row(packed, 0).astype(BF16)
    gout_row = as_row(packed, ROWS).astype(BF16)
    loads[2].wait()
    pre_act = dot(slot_row, win[...])
    gelu_value, gelu_slope = gelu_parts(pre_act)
    loads[3].wait()
    grad_hidden = tail_dot(gout_row, wout[...])
    slot_out = dot(gelu_value.astype(BF16), wout[...])
    grad_in = tail_dot((grad_hidden * gelu_slope).astype(BF16), win[...])
    for j in range(ROWS):
        rows_s[j : j + 1, :] = slot_out[:, 128 * j : 128 * (j + 1)]
        rows_s[ROWS + j : ROWS + j + 1, :] = grad_in[:, 128 * j : 128 * (j + 1)]
    out_b[...] = rows_s[...].astype(BF16)
    disp_inner = jnp.sum(packed[:ROWS, :] * out_b[...].astype(F32)[ROWS:, :])
    lane = lax.broadcasted_iota(jnp.int32, (1, 128), 1)
    stat_own[...] = jnp.where(
        lane == 0, high[0], jnp.where(lane == 1, stat_sum[:, 1:2], disp_inner)
    )
    sg[me] = out_b[...]
    stat[me] = stat_own[...]

    send(4, place_peer, lambda p: sg.at[me], sg.at[me])
    send(5, place_peer, lambda p: stat.at[me], stat.at[me])
    landed(4, sg.at[pl.ds(0, 7)])
    landed(5, stat.at[pl.ds(0, 7)])
    block = pl.ds(pl.multiple_of(group * 8, 8), 8)
    send(6, group_peer, lambda p: sg.at[block], sg.at[block])
    send(7, group_peer, lambda p: stat.at[block], stat.at[block])
    landed(6, sg.at[pl.ds(0, 56)])
    landed(7, stat.at[pl.ds(0, 56)])
    sg_f[...] = sg[...].astype(F32).reshape(SLOTS * 16, 128)
    outs = jnp.concatenate(
        [sg_f[pl.ds(j, SLOTS, stride=16), :].astype(BF16) for j in range(ROWS)], axis=1
    )
    for j in range(ROWS):
        key_in[:SLOTS, 128 * j : 128 * (j + 1)] = sg_f[pl.ds(ROWS + j, SLOTS, stride=16), :].astype(BF16)

    stats = stat[...].reshape(SLOTS, 128)
    grad_comb = tail_dot(outs, cot[...])
    comb = comb_s[...]
    comb_inner = jnp.sum(comb * grad_comb, axis=0, keepdims=True)
    logit_grad = comb * (grad_comb - comb_inner)
    grad_disp = tail_dot(key_in[:SLOTS, :], tok[...])
    peak = part[:, 2 * D : 2 * D + 1]
    dispatch = ex_s[...] * (jnp.exp(peak - stats[:, 0:1]) / stats[:, 1:2])
    logit_grad = logit_grad + dispatch * (grad_disp - stats[:, 2:3])
    coef[:SLOTS, :] = dispatch.astype(BF16)
    coef[SLOTS:, :] = logit_grad.astype(BF16)
    back[...] = dot(coef[SLOTS:, :], tok[...])

    send(8, group_peer, lambda g: back.at[eight(g)], land3.at[group])
    land3[group] = back[eight(group), :]
    gtok_ref[...] = lead_dot(coef[...], key_in[...]).astype(BF16)
    landed(8, land3.at[pl.ds(0, 7)])
    back_sum = jnp.sum(land3[...], axis=0)
    for j in range(ROWS):
        back2[pl.ds(j, 8, stride=8), :] = back_sum[:, 128 * j : 128 * (j + 1)]
    send(9, place_peer, lambda p: back2.at[eight(p)], land4.at[place])
    land4[place] = back2[eight(place), :]
    mixed_ref[...] = lead_dot(combb_s[...], outs).astype(BF16)
    landed(9, land4.at[pl.ds(0, 7)])
    grout_ref[...] = jnp.sum(land4[...], axis=0)

    sent(0, keys.at[pl.ds(0, 56)])
    sent(1, keys.at[pl.ds(0, 448)])
    sent(2, land1.at[pl.ds(0, 7)])
    sent(3, land2.at[pl.ds(0, 7)])
    sent(4, sg.at[pl.ds(0, 7)])
    sent(5, stat.at[pl.ds(0, 7)])
    sent(6, sg.at[pl.ds(0, 56)])
    sent(7, stat.at[pl.ds(0, 56)])
    sent(8, land3.at[pl.ds(0, 7)])
    sent(9, land4.at[pl.ds(0, 7)])


def body(tokens, router, w_in, w_out, cotangent):
    anywhere = pl.BlockSpec(memory_space=pl.ANY)
    vmem = pl.BlockSpec(memory_space=pltpu.VMEM)
    v = pltpu.VMEM
    mixed, grad_tokens, grad_router = pl.pallas_call(
        kernel,
        out_shape=(
            jax.ShapeDtypeStruct((TOK, D), BF16),
            jax.ShapeDtypeStruct((TOK, D), BF16),
            jax.ShapeDtypeStruct((ROWS, 128), F32),
        ),
        in_specs=[anywhere, vmem, anywhere, anywhere, anywhere],
        out_specs=[vmem, vmem, vmem],
        scratch_shapes=[
            v((TOK, D), BF16), v((TOK, D), BF16), v((D, H), BF16), v((H, D), BF16),
            v((ROWS, 128), F32), v((SLOTS * ROWS, 128), F32), v((2 * SLOTS, D), BF16),
            v((SLOTS, TOK), F32), v((SLOTS, TOK), F32), v((SLOTS, TOK), BF16),
            v((SLOTS, WIDE), F32), v((GROUPS, 8, WIDE), F32),
            v((PLACES * PACK, 128), F32), v((PLACES, PACK, 128), F32),
            v((2 * ROWS, 128), F32), v((2 * ROWS, 128), F32),
            v((SLOTS, 2 * ROWS, 128), BF16), v((SLOTS * 2 * ROWS, 128), F32),
            v((SLOTS, 1, 128), F32), v((1, 128), F32), v((2 * ROWS, 128), BF16),
            v((SLOTS, D), F32), v((GROUPS, 8, D), F32),
            v((PLACES * ROWS, 128), F32), v((PLACES, ROWS, 128), F32),
            v((2 * SLOTS, TOK), BF16),
            pltpu.SemaphoreType.DMA((4,)),
            pltpu.SemaphoreType.DMA((10,)), pltpu.SemaphoreType.DMA((10,)),
        ],
        compiler_params=pltpu.CompilerParams(
            collective_id=0, has_side_effects=True, vmem_limit_bytes=40 << 20
        ),
    )(tokens, router, w_in, w_out, cotangent)
    return (mixed, grad_tokens, grad_router.reshape(1, D))


def solution(mesh):
    return jax.shard_map(
        body,
        mesh=mesh,
        in_specs=(
            P(("batch", "seq"), None),
            P("seq", None),
            P("seq", None, None),
            P("seq", None, None),
            P(("batch", "seq"), None),
        ),
        out_specs=(P(("batch", "seq"), None), P(("batch", "seq"), None), P(("batch", "seq"), None)),
        check_vma=False,
    )
```

```python
import functools

import jax
import jax.numpy as jnp
from jax import lax
from jax.experimental import pallas as pl
from jax.experimental.pallas import tpu as pltpu
from jax.sharding import PartitionSpec as P

GELU_C = 0.7978845608028654
GELU_K = 0.044715
MESH = pl.DeviceIdType.MESH
F32, BF16 = jnp.float32, jnp.bfloat16

GROUPS, PLACES = 8, 8
SLOTS = GROUPS * PLACES
TOK = 512
D = 1024
H = 2048
ROWS = D // 128
WIDE = D + 128
PACK = 2 * ROWS
FAR = (2, 1, 3, 0)


def gelu_parts(pre_act):
    inner = GELU_C * (pre_act + GELU_K * pre_act * pre_act * pre_act)
    tanh_v = jnp.tanh(inner)
    gelu_value = 0.5 * pre_act * (1.0 + tanh_v)
    gelu_slope = 0.5 * (1.0 + tanh_v) + 0.5 * pre_act * (1.0 - tanh_v * tanh_v) * GELU_C * (
        1.0 + 3.0 * GELU_K * pre_act * pre_act
    )
    return (gelu_value, gelu_slope)


def dot(left, right):
    return jnp.dot(left, right, preferred_element_type=F32)


def tail_dot(left, right):
    return lax.dot_general(left, right, (((1,), (1,)), ((), ())), preferred_element_type=F32)


def lead_dot(left, right):
    return lax.dot_general(left, right, (((0,), (0,)), ((), ())), preferred_element_type=F32)


def as_row(ref, first):
    return jnp.concatenate([ref[first + j : first + j + 1, :] for j in range(ROWS)], axis=1)


def split3(value):
    high = value.astype(BF16).astype(F32)
    middle = (value - high).astype(BF16).astype(F32)
    return high, middle, value - high - middle


def kernel(
    tok_h, router_h, win_h, wout_h, cot_h,
    mixed_ref, gtok_ref, grout_ref,
    tok, cot, win, wout, key_own, own, keys, keys_f, key_in,
    ex_s, comb_s, combb_s, part, gpart, land1, gland1, pack, gpack, land2, gland2, packed, rows_s,
    s_all, g_all, g_f, outs, back, land3, coef,
    load_sem, send_sem, recv_sem,
):
    me = lax.axis_index("seq")
    group, place = me // PLACES, lax.rem(me, PLACES)

    loads = [
        pltpu.make_async_copy(src, dst, load_sem.at[i])
        for i, (src, dst) in enumerate(
            ((router_h, key_own), (tok_h, tok), (cot_h, cot), (win_h.at[0], win), (wout_h.at[0], wout))
        )
    ]
    for load in loads:
        load.start()

    side, along = group // 4, lax.rem(group, 4)
    far_groups = [
        lax.rem(side + 1 - c // 4, 2) * 4 + lax.rem(along + FAR[c % 4], 4) for c in range(8)
    ]
    far_places = [lax.rem(place + k, PLACES) for k in (4, 3, 5, 2, 6, 1, 7)]

    def everyone(act):
        def some(i, carry):
            step = (i + 1) // 2
            p = lax.rem(place + 4 + step * (1 - 2 * lax.rem(i, 2)), PLACES)
            for g in far_groups:
                act(g * PLACES + p)
            return carry

        lax.fori_loop(0, 7, some, 0)
        for g in far_groups[:7]:
            act(g * PLACES + place)

    barrier = pltpu.get_barrier_semaphore()
    everyone(
        lambda p: pl.semaphore_signal(barrier, inc=1, device_id={"seq": p}, device_id_type=MESH)
    )

    def put(stage, src, dst, peer):
        pltpu.make_async_remote_copy(
            src_ref=src, dst_ref=dst,
            send_sem=send_sem.at[stage], recv_sem=recv_sem.at[stage],
            device_id={"seq": peer}, device_id_type=MESH,
        ).start()

    def landed(stage, others):
        pltpu.make_async_copy(others, others, recv_sem.at[stage]).wait()

    def sent(stage, others):
        pltpu.make_async_copy(others, others, send_sem.at[stage]).wait()

    def eight(first):
        return pl.ds(pl.multiple_of(first * 8, 8), 8)

    def strip(first):
        return pl.ds(pl.multiple_of(first * PACK, 8), 9)

    loads[0].wait()
    key_row = key_own[...].astype(F32)
    for j in range(ROWS):
        own[j : j + 1, :] = key_row[:, 128 * j : 128 * (j + 1)]
    keys[me] = own[...].astype(BF16)
    pl.semaphore_wait(barrier, SLOTS - 1)
    everyone(lambda p: put(0, keys.at[me], keys.at[me], p))
    landed(0, keys.at[pl.ds(0, SLOTS - 1)])
    keys_f[...] = keys[...].astype(F32).reshape(SLOTS * ROWS, 128)
    for j in range(ROWS):
        key_in[SLOTS:, 128 * j : 128 * (j + 1)] = keys_f[pl.ds(j, SLOTS, stride=8), :].astype(BF16)

    loads[1].wait()
    logit_t = tail_dot(key_in[SLOTS:, :], tok[...])
    peak = jnp.max(logit_t, axis=1, keepdims=True)
    ex = jnp.exp(logit_t - peak)
    ex_s[...] = ex
    ex_b = ex.astype(BF16)
    total = jnp.sum(ex, axis=1, keepdims=True)
    total_b = jnp.sum(ex_b.astype(F32), axis=1, keepdims=True)
    lane = lax.broadcasted_iota(jnp.int32, (SLOTS, 128), 1)
    part[:, D:] = jnp.where(lane == 0, peak, jnp.where(lane == 1, total, total_b))
    part[:, :D] = dot(ex_b, tok[...])
    for g in far_groups[:7]:
        put(1, part.at[eight(g)], land1.at[group], g * PLACES + place)
    land1[group] = part[eight(group), :]

    row_peak = jnp.max(logit_t, axis=0, keepdims=True)
    row_ex = jnp.exp(logit_t - row_peak)
    comb = row_ex / jnp.sum(row_ex, axis=0, keepdims=True)
    comb_s[...] = comb
    combb_s[...] = comb.astype(BF16)
    loads[2].wait()
    gpart[...] = dot(combb_s[...], cot[...])
    for g in far_groups[:7]:
        put(2, gpart.at[eight(g)], gland1.at[group], g * PLACES + place)
    gland1[group] = gpart[eight(group), :]

    landed(1, land1.at[pl.ds(0, 7)])
    peaks = land1[:, :, D : D + 1]
    high = jnp.max(peaks, axis=0, keepdims=True)
    scale = jnp.exp(peaks - high)
    slot_sum = jnp.sum(land1[:, :, :D] * scale, axis=0)
    stat_sum = jnp.sum(land1[:, :, D:] * scale, axis=0)
    lane = lax.broadcasted_iota(jnp.int32, (8, 128), 1)
    stat_sum = jnp.where(lane == 0, high[0], stat_sum)
    for j in range(ROWS):
        pack[pl.ds(j, 8, stride=PACK), :] = slot_sum[:, 128 * j : 128 * (j + 1)]
    pack[pl.ds(ROWS, 8, stride=PACK), :] = stat_sum
    for p in far_places:
        put(3, pack.at[strip(p)], land2.at[place, pl.ds(0, 9)], group * PLACES + p)
    land2[place, :9] = pack[strip(place), :]
    landed(2, gland1.at[pl.ds(0, 7)])
    gout_sum = jnp.sum(gland1[...], axis=0)
    for j in range(ROWS):
        gpack[pl.ds(j, 8, stride=ROWS), :] = gout_sum[:, 128 * j : 128 * (j + 1)]
    for p in far_places:
        put(4, gpack.at[eight(p)], gland2.at[place], group * PLACES + p)
    gland2[place] = gpack[eight(place), :]

    landed(3, land2.at[pl.ds(0, 7), pl.ds(0, 9)])
    peaks = land2[:, ROWS : ROWS + 1, 0:1]
    high = jnp.max(peaks, axis=0, keepdims=True)
    scale = jnp.exp(peaks - high)
    stat_sum = jnp.sum(land2[:, ROWS : ROWS + 1, :] * scale, axis=0)
    packed[:ROWS, :] = jnp.sum(land2[:, :ROWS, :] * scale, axis=0) / stat_sum[:, 2:3]
    slot_row = as_row(packed, 0).astype(BF16)
    loads[3].wait()
    gelu_value, gelu_slope = gelu_parts(dot(slot_row, win[...]))
    loads[4].wait()
    slot_out = dot(gelu_value.astype(BF16), wout[...])
    for j in range(ROWS):
        rows_s[j : j + 1, :] = slot_out[:, 128 * j : 128 * (j + 1)]
    s_all[me] = rows_s[:ROWS, :].astype(BF16)
    everyone(lambda p: put(5, s_all.at[me], s_all.at[me], p))

    landed(4, gland2.at[pl.ds(0, 7)])
    packed[ROWS:, :] = jnp.sum(gland2[...], axis=0)
    gout_row = as_row(packed, ROWS).astype(BF16)
    grad_pre = (tail_dot(gout_row, wout[...]) * gelu_slope).astype(BF16)
    grad_in = tail_dot(grad_pre, win[...]).astype(BF16).astype(F32)
    for j in range(ROWS):
        rows_s[j : j + 1, :] = grad_in[:, 128 * j : 128 * (j + 1)]
    disp_inner = jnp.sum(packed[:ROWS, :] * rows_s[:ROWS, :])
    lane = lax.broadcasted_iota(jnp.int32, (1, 128), 1)
    stat = jnp.where(lane == 0, high[0], jnp.where(lane == 1, stat_sum[:, 1:2], disp_inner))
    for j, third in enumerate(split3(stat)):
        rows_s[ROWS + j : ROWS + j + 1, :] = third
    g_all[me] = rows_s[...].astype(BF16)
    everyone(lambda p: put(6, g_all.at[me], g_all.at[me], p))

    landed(5, s_all.at[pl.ds(0, SLOTS - 1)])
    keys_f[...] = s_all[...].astype(F32).reshape(SLOTS * ROWS, 128)
    for j in range(ROWS):
        outs[:, 128 * j : 128 * (j + 1)] = keys_f[pl.ds(j, SLOTS, stride=8), :].astype(BF16)
    grad_comb = tail_dot(outs[...], cot[...])
    comb = comb_s[...]
    comb_inner = jnp.sum(comb * grad_comb, axis=0, keepdims=True)
    logit_grad = comb * (grad_comb - comb_inner)

    landed(6, g_all.at[pl.ds(0, SLOTS - 1)])
    g_f[...] = g_all[...].astype(F32).reshape(SLOTS * PACK, 128)
    for j in range(ROWS):
        key_in[:SLOTS, 128 * j : 128 * (j + 1)] = g_f[pl.ds(j, SLOTS, stride=PACK), :].astype(BF16)
    stats = (
        g_f[pl.ds(ROWS, SLOTS, stride=PACK), :]
        + g_f[pl.ds(ROWS + 1, SLOTS, stride=PACK), :]
        + g_f[pl.ds(ROWS + 2, SLOTS, stride=PACK), :]
    )
    grad_disp = tail_dot(key_in[:SLOTS, :], tok[...])
    peak = part[:, D : D + 1]
    dispatch = ex_s[...] * (jnp.exp(peak - stats[:, 0:1]) / stats[:, 1:2])
    logit_grad = logit_grad + dispatch * (grad_disp - stats[:, 2:3])
    coef[:SLOTS, :] = dispatch.astype(BF16)
    coef[SLOTS:, :] = logit_grad.astype(BF16)
    key_grad = dot(coef[SLOTS:, :], tok[...])
    for j in range(ROWS):
        back[pl.ds(j, SLOTS, stride=8), :] = key_grad[:, 128 * j : 128 * (j + 1)]

    everyone(lambda p: put(7, back.at[eight(p)], land3.at[me], p))
    land3[me] = back[eight(me), :]
    gtok_ref[...] = lead_dot(coef[...], key_in[...]).astype(BF16)
    mixed_ref[...] = lead_dot(combb_s[...], outs[...]).astype(BF16)
    landed(7, land3.at[pl.ds(0, SLOTS - 1)])
    grout_ref[...] = jnp.sum(land3[...], axis=0)

    sent(0, keys.at[pl.ds(0, SLOTS - 1)])
    sent(1, land1.at[pl.ds(0, 7)])
    sent(2, gland1.at[pl.ds(0, 7)])
    sent(3, land2.at[pl.ds(0, 7), pl.ds(0, 9)])
    sent(4, gland2.at[pl.ds(0, 7)])
    sent(5, s_all.at[pl.ds(0, SLOTS - 1)])
    sent(6, g_all.at[pl.ds(0, SLOTS - 1)])
    sent(7, land3.at[pl.ds(0, SLOTS - 1)])


def body(tokens, router, w_in, w_out, cotangent):
    hbm = pl.BlockSpec(memory_space=pltpu.HBM)
    vmem = pl.BlockSpec(memory_space=pltpu.VMEM)
    v = pltpu.VMEM
    mixed, grad_tokens, grad_router = pl.pallas_call(
        kernel,
        out_shape=(v((TOK, D), BF16), v((TOK, D), BF16), v((ROWS, 128), F32)),
        in_specs=[hbm] * 5,
        out_specs=[vmem, vmem, vmem],
        scratch_shapes=[
            v((TOK, D), BF16), v((TOK, D), BF16), v((D, H), BF16), v((H, D), BF16),
            v((1, D), BF16), v((ROWS, 128), F32), v((SLOTS, ROWS, 128), BF16),
            v((SLOTS * ROWS, 128), F32), v((2 * SLOTS, D), BF16),
            v((SLOTS, TOK), F32), v((SLOTS, TOK), F32), v((SLOTS, TOK), BF16),
            v((SLOTS, WIDE), F32), v((SLOTS, D), F32),
            v((GROUPS, 8, WIDE), F32), v((GROUPS, 8, D), F32),
            v((PLACES * PACK, 128), F32), v((PLACES * ROWS, 128), F32),
            v((PLACES, PACK, 128), F32), v((PLACES, ROWS, 128), F32),
            v((2 * ROWS, 128), F32), v((2 * ROWS, 128), F32),
            v((SLOTS, ROWS, 128), BF16), v((SLOTS, PACK, 128), BF16), v((SLOTS * PACK, 128), F32),
            v((SLOTS, D), BF16), v((SLOTS * ROWS, 128), F32), v((SLOTS, ROWS, 128), F32),
            v((2 * SLOTS, TOK), BF16),
            pltpu.SemaphoreType.DMA((5,)),
            pltpu.SemaphoreType.DMA((8,)), pltpu.SemaphoreType.DMA((8,)),
        ],
        compiler_params=pltpu.CompilerParams(
            collective_id=0, has_side_effects=True, vmem_limit_bytes=60 << 20
        ),
    )(tokens, router, w_in, w_out, cotangent)
    return (mixed, grad_tokens, grad_router.reshape(1, D))


def solution(mesh):
    return jax.shard_map(
        body,
        mesh=mesh,
        in_specs=(
            P(("batch", "seq"), None),
            P("seq", None),
            P("seq", None, None),
            P("seq", None, None),
            P(("batch", "seq"), None),
        ),
        out_specs=(P(("batch", "seq"), None), P(("batch", "seq"), None), P(("batch", "seq"), None)),
        check_vma=False,
    )
```

```python
import functools

import jax
import jax.numpy as jnp
from jax import lax
from jax.experimental import pallas as pl
from jax.experimental.pallas import tpu as pltpu
from jax.sharding import PartitionSpec as P

GELU_C = 0.7978845608028654
GELU_K = 0.044715
MESH = pl.DeviceIdType.MESH
F32, BF16 = jnp.float32, jnp.bfloat16

GROUPS, PLACES = 8, 8
SLOTS = GROUPS * PLACES
TOK = 512
D = 1024
H = 2048
ROWS = D // 128
HALF = D // 2
PACK = 2 * ROWS
FAR = (2, 1, 3, 0)


def gelu_parts(pre_act):
    inner = GELU_C * (pre_act + GELU_K * pre_act * pre_act * pre_act)
    tanh_v = jnp.tanh(inner)
    gelu_value = 0.5 * pre_act * (1.0 + tanh_v)
    gelu_slope = 0.5 * (1.0 + tanh_v) + 0.5 * pre_act * (1.0 - tanh_v * tanh_v) * GELU_C * (
        1.0 + 3.0 * GELU_K * pre_act * pre_act
    )
    return (gelu_value, gelu_slope)


def dot(left, right):
    return jnp.dot(left, right, preferred_element_type=F32)


def tail_dot(left, right):
    return lax.dot_general(left, right, (((1,), (1,)), ((), ())), preferred_element_type=F32)


def lead_dot(left, right):
    return lax.dot_general(left, right, (((0,), (0,)), ((), ())), preferred_element_type=F32)


def as_row(ref, first):
    return jnp.concatenate([ref[first + j : first + j + 1, :] for j in range(ROWS)], axis=1)


def kernel(
    tok_h, router_h, win_h, wout_h, cot_h,
    mixed_ref, gtok_ref, grout_ref,
    tok, cot, win, wout, key_own, own, keys, keys_f, key_in,
    ex_s, comb_s, combb_s, stat, part, gpart, stat1, land1, gland1, pack, gpack, land2, gland2,
    packed, rows_s, stat_all, sg_all, sg_f, outs, back, land3, coef,
    load_sem, send_sem, recv_sem,
):
    me = lax.axis_index("seq")
    group, place = me // PLACES, lax.rem(me, PLACES)

    loads = [
        pltpu.make_async_copy(src, dst, load_sem.at[i])
        for i, (src, dst) in enumerate(
            ((router_h, key_own), (tok_h, tok), (cot_h, cot), (win_h.at[0], win), (wout_h.at[0], wout))
        )
    ]
    for load in loads:
        load.start()

    side, along = group // 4, lax.rem(group, 4)
    far_groups = [
        lax.rem(side + 1 - c // 4, 2) * 4 + lax.rem(along + FAR[c % 4], 4) for c in range(8)
    ]
    far_places = [lax.rem(place + k, PLACES) for k in (4, 3, 5, 2, 6, 1, 7)]

    def everyone(act):
        def some(i, carry):
            step = (i + 1) // 2
            p = lax.rem(place + 4 + step * (1 - 2 * lax.rem(i, 2)), PLACES)
            for g in far_groups:
                act(g * PLACES + p)
            return carry

        lax.fori_loop(0, 7, some, 0)
        for g in far_groups[:7]:
            act(g * PLACES + place)

    barrier = pltpu.get_barrier_semaphore()
    everyone(
        lambda p: pl.semaphore_signal(barrier, inc=1, device_id={"seq": p}, device_id_type=MESH)
    )

    def put(stage, src, dst, peer):
        pltpu.make_async_remote_copy(
            src_ref=src, dst_ref=dst,
            send_sem=send_sem.at[stage], recv_sem=recv_sem.at[stage],
            device_id={"seq": peer}, device_id_type=MESH,
        ).start()

    def landed(stage, others):
        pltpu.make_async_copy(others, others, recv_sem.at[stage]).wait()

    def sent(stage, others):
        pltpu.make_async_copy(others, others, send_sem.at[stage]).wait()

    def halves(ref, value):
        for g in range(GROUPS):
            rows = value[8 * g : 8 * g + 8, :]
            ref[g] = jnp.concatenate([rows[:, :HALF], rows[:, HALF:]], axis=0).astype(BF16)

    def lay(ref, value, stride):
        for j in range(ROWS):
            row, column = 8 * (j // 4), 128 * (j % 4)
            ref[pl.ds(j, 8, stride=stride), :] = value[row : row + 8, column : column + 128]

    def eight(first):
        return pl.ds(pl.multiple_of(first * 8, 8), 8)

    def strip(first):
        return pl.ds(pl.multiple_of(first * PACK, 8), 9)

    loads[0].wait()
    key_row = key_own[...].astype(F32)
    for j in range(ROWS):
        own[j : j + 1, :] = key_row[:, 128 * j : 128 * (j + 1)]
    keys[me] = own[...].astype(BF16)
    pl.semaphore_wait(barrier, SLOTS - 1)
    everyone(lambda p: put(0, keys.at[me], keys.at[me], p))
    landed(0, keys.at[pl.ds(0, SLOTS - 1)])
    keys_f[...] = keys[...].astype(F32).reshape(SLOTS * ROWS, 128)
    for j in range(ROWS):
        key_in[SLOTS:, 128 * j : 128 * (j + 1)] = keys_f[pl.ds(j, SLOTS, stride=8), :].astype(BF16)

    loads[1].wait()
    logit_t = tail_dot(key_in[SLOTS:, :], tok[...])
    peak = jnp.max(logit_t, axis=1, keepdims=True)
    ex = jnp.exp(logit_t - peak)
    ex_s[...] = ex
    ex_b = ex.astype(BF16)
    total = jnp.sum(ex, axis=1, keepdims=True)
    total_b = jnp.sum(ex_b.astype(F32), axis=1, keepdims=True)
    lane = lax.broadcasted_iota(jnp.int32, (SLOTS, 128), 1)
    stat[...] = jnp.where(lane == 0, peak, jnp.where(lane == 1, total, total_b))
    for g in far_groups[:7]:
        put(1, stat.at[eight(g)], stat1.at[group], g * PLACES + place)
    stat1[group] = stat[eight(group), :]
    halves(part, dot(ex_b, tok[...]))
    for g in far_groups[:7]:
        put(2, part.at[g], land1.at[group], g * PLACES + place)
    land1[group] = part[group]

    row_peak = jnp.max(logit_t, axis=0, keepdims=True)
    row_ex = jnp.exp(logit_t - row_peak)
    comb = row_ex / jnp.sum(row_ex, axis=0, keepdims=True)
    comb_s[...] = comb
    combb_s[...] = comb.astype(BF16)
    loads[2].wait()
    halves(gpart, dot(combb_s[...], cot[...]))
    for g in far_groups[:7]:
        put(3, gpart.at[g], gland1.at[group], g * PLACES + place)
    gland1[group] = gpart[group]

    landed(1, stat1.at[pl.ds(0, 7)])
    peaks = stat1[:, :, 0:1]
    high = jnp.max(peaks, axis=0, keepdims=True)
    scale = jnp.exp(peaks - high)
    stat_sum = jnp.sum(stat1[...] * scale, axis=0)
    lane = lax.broadcasted_iota(jnp.int32, (8, 128), 1)
    pack[pl.ds(ROWS, 8, stride=PACK), :] = jnp.where(lane == 0, high[0], stat_sum)
    landed(2, land1.at[pl.ds(0, 7)])
    twice = jnp.concatenate([scale, scale], axis=1)
    lay(pack, jnp.sum(land1[...].astype(F32) * twice, axis=0), PACK)
    for p in far_places:
        put(4, pack.at[strip(p)], land2.at[place, pl.ds(0, 9)], group * PLACES + p)
    land2[place, :9] = pack[strip(place), :]
    landed(3, gland1.at[pl.ds(0, 7)])
    lay(gpack, jnp.sum(gland1[...].astype(F32), axis=0), ROWS)
    for p in far_places:
        put(5, gpack.at[eight(p)], gland2.at[place], group * PLACES + p)
    gland2[place] = gpack[eight(place), :]

    landed(4, land2.at[pl.ds(0, 7), pl.ds(0, 9)])
    peaks = land2[:, ROWS : ROWS + 1, 0:1]
    high = jnp.max(peaks, axis=0, keepdims=True)
    scale = jnp.exp(peaks - high)
    stat_sum = jnp.sum(land2[:, ROWS : ROWS + 1, :] * scale, axis=0)
    packed[:ROWS, :] = jnp.sum(land2[:, :ROWS, :] * scale, axis=0) / stat_sum[:, 2:3]
    slot_row = as_row(packed, 0).astype(BF16)
    loads[3].wait()
    gelu_value, gelu_slope = gelu_parts(dot(slot_row, win[...]))
    loads[4].wait()
    slot_out = dot(gelu_value.astype(BF16), wout[...])
    for j in range(ROWS):
        rows_s[j : j + 1, :] = slot_out[:, 128 * j : 128 * (j + 1)]

    landed(5, gland2.at[pl.ds(0, 7)])
    packed[ROWS:, :] = jnp.sum(gland2[...], axis=0)
    gout_row = as_row(packed, ROWS).astype(BF16)
    grad_pre = (tail_dot(gout_row, wout[...]) * gelu_slope).astype(BF16)
    grad_in = tail_dot(grad_pre, win[...]).astype(BF16).astype(F32)
    for j in range(ROWS):
        rows_s[ROWS + j : ROWS + j + 1, :] = grad_in[:, 128 * j : 128 * (j + 1)]
    sg_all[me] = rows_s[...].astype(BF16)
    disp_inner = jnp.sum(packed[:ROWS, :] * rows_s[ROWS:, :])
    lane = lax.broadcasted_iota(jnp.int32, (1, 128), 1)
    stat_all[me] = jnp.where(
        lane == 0, high[0], jnp.where(lane == 1, stat_sum[:, 1:2], disp_inner)
    )
    for p in far_places:
        put(6, stat_all.at[me], stat_all.at[me], group * PLACES + p)
    everyone(lambda p: put(7, sg_all.at[me], sg_all.at[me], p))
    landed(6, stat_all.at[pl.ds(0, 7)])
    mates = eight(group)
    for g in far_groups[:7]:
        put(8, stat_all.at[mates], stat_all.at[mates], g * PLACES + place)

    landed(7, sg_all.at[pl.ds(0, SLOTS - 1)])
    sg_f[...] = sg_all[...].astype(F32).reshape(SLOTS * PACK, 128)
    for j in range(ROWS):
        columns = slice(128 * j, 128 * (j + 1))
        outs[:, columns] = sg_f[pl.ds(j, SLOTS, stride=PACK), :].astype(BF16)
        key_in[:SLOTS, columns] = sg_f[pl.ds(ROWS + j, SLOTS, stride=PACK), :].astype(BF16)
    grad_comb = tail_dot(outs[...], cot[...])
    comb = comb_s[...]
    comb_inner = jnp.sum(comb * grad_comb, axis=0, keepdims=True)
    logit_grad = comb * (grad_comb - comb_inner)
    grad_disp = tail_dot(key_in[:SLOTS, :], tok[...])
    landed(8, stat_all.at[pl.ds(0, 56)])
    stats = stat_all[...].reshape(SLOTS, 128)
    dispatch = ex_s[...] * (jnp.exp(stat[:, 0:1] - stats[:, 0:1]) / stats[:, 1:2])
    logit_grad = logit_grad + dispatch * (grad_disp - stats[:, 2:3])
    coef[:SLOTS, :] = dispatch.astype(BF16)
    coef[SLOTS:, :] = logit_grad.astype(BF16)
    key_grad = dot(coef[SLOTS:, :], tok[...])
    for j in range(ROWS):
        back[pl.ds(j, SLOTS, stride=8), :] = key_grad[:, 128 * j : 128 * (j + 1)]

    everyone(lambda p: put(9, back.at[eight(p)], land3.at[me], p))
    land3[me] = back[eight(me), :]
    gtok_ref[...] = lead_dot(coef[...], key_in[...]).astype(BF16)
    mixed_ref[...] = lead_dot(combb_s[...], outs[...]).astype(BF16)
    landed(9, land3.at[pl.ds(0, SLOTS - 1)])
    grout_ref[...] = jnp.sum(land3[...], axis=0)

    sent(0, keys.at[pl.ds(0, SLOTS - 1)])
    sent(1, stat1.at[pl.ds(0, 7)])
    sent(2, land1.at[pl.ds(0, 7)])
    sent(3, gland1.at[pl.ds(0, 7)])
    sent(4, land2.at[pl.ds(0, 7), pl.ds(0, 9)])
    sent(5, gland2.at[pl.ds(0, 7)])
    sent(6, stat_all.at[pl.ds(0, 7)])
    sent(7, sg_all.at[pl.ds(0, SLOTS - 1)])
    sent(8, stat_all.at[pl.ds(0, 56)])
    sent(9, land3.at[pl.ds(0, SLOTS - 1)])


def store_kernel(mixed_ref, gtok_ref, grout_ref, mixed_out, gtok_out, grout_out, row, sems):
    stores = [
        pltpu.make_async_copy(mixed_ref, mixed_out, sems.at[0]),
        pltpu.make_async_copy(gtok_ref, gtok_out, sems.at[1]),
    ]
    for store in stores:
        store.start()
    row[...] = jnp.concatenate([grout_ref[j : j + 1, :] for j in range(ROWS)], axis=1)
    last = pltpu.make_async_copy(row, grout_out, sems.at[2])
    last.start()
    for store in stores:
        store.wait()
    last.wait()


def body(tokens, router, w_in, w_out, cotangent):
    anywhere = pl.BlockSpec(memory_space=pl.ANY)
    hbm = pl.BlockSpec(memory_space=pltpu.HBM)
    vmem = pl.BlockSpec(memory_space=pltpu.VMEM)
    v = pltpu.VMEM
    mixed, grad_tokens, grad_router = pl.pallas_call(
        kernel,
        out_shape=(v((TOK, D), BF16), v((TOK, D), BF16), v((ROWS, 128), F32)),
        in_specs=[hbm] * 5,
        out_specs=[vmem, vmem, vmem],
        scratch_shapes=[
            v((TOK, D), BF16), v((TOK, D), BF16), v((D, H), BF16), v((H, D), BF16),
            v((1, D), BF16), v((ROWS, 128), F32), v((SLOTS, ROWS, 128), BF16),
            v((SLOTS * ROWS, 128), F32), v((2 * SLOTS, D), BF16),
            v((SLOTS, TOK), F32), v((SLOTS, TOK), F32), v((SLOTS, TOK), BF16),
            v((SLOTS, 128), F32), v((GROUPS, 16, HALF), BF16), v((GROUPS, 16, HALF), BF16),
            v((GROUPS, 8, 128), F32), v((GROUPS, 16, HALF), BF16), v((GROUPS, 16, HALF), BF16),
            v((PLACES * PACK, 128), F32), v((PLACES * ROWS, 128), F32),
            v((PLACES, PACK, 128), F32), v((PLACES, ROWS, 128), F32),
            v((2 * ROWS, 128), F32), v((2 * ROWS, 128), F32),
            v((SLOTS, 1, 128), F32), v((SLOTS, PACK, 128), BF16), v((SLOTS * PACK, 128), F32),
            v((SLOTS, D), BF16), v((SLOTS * ROWS, 128), F32), v((SLOTS, ROWS, 128), F32),
            v((2 * SLOTS, TOK), BF16),
            pltpu.SemaphoreType.DMA((5,)),
            pltpu.SemaphoreType.DMA((10,)), pltpu.SemaphoreType.DMA((10,)),
        ],
        compiler_params=pltpu.CompilerParams(
            collective_id=0, has_side_effects=True, vmem_limit_bytes=60 << 20
        ),
    )(tokens, router, w_in, w_out, cotangent)
    return pl.pallas_call(
        store_kernel,
        out_shape=(
            jax.ShapeDtypeStruct((TOK, D), BF16),
            jax.ShapeDtypeStruct((TOK, D), BF16),
            jax.ShapeDtypeStruct((1, D), F32),
        ),
        in_specs=[vmem] * 3,
        out_specs=[anywhere, anywhere, anywhere],
        scratch_shapes=[v((1, D), F32), pltpu.SemaphoreType.DMA((3,))],
        compiler_params=pltpu.CompilerParams(vmem_limit_bytes=1 << 20),
    )(mixed, grad_tokens, grad_router)


def solution(mesh):
    return jax.shard_map(
        body,
        mesh=mesh,
        in_specs=(
            P(("batch", "seq"), None),
            P("seq", None),
            P("seq", None, None),
            P("seq", None, None),
            P(("batch", "seq"), None),
        ),
        out_specs=(P(("batch", "seq"), None), P(("batch", "seq"), None), P(("batch", "seq"), None)),
        check_vma=False,
    )
```

```python
import functools

import jax
import jax.numpy as jnp
from jax import lax
from jax.experimental import pallas as pl
from jax.experimental.pallas import tpu as pltpu
from jax.sharding import PartitionSpec as P

GELU_C = 0.7978845608028654
GELU_K = 0.044715
MESH = pl.DeviceIdType.MESH
F32, BF16 = jnp.float32, jnp.bfloat16

GROUPS, PLACES = 8, 8
SLOTS = GROUPS * PLACES
TOK = 512
D = 1024
H = 2048
ROWS = D // 128
HALF = D // 2
PACK = 2 * ROWS
FAR = (2, 1, 3, 0)


def gelu_parts(pre_act):
    inner = GELU_C * (pre_act + GELU_K * pre_act * pre_act * pre_act)
    tanh_v = jnp.tanh(inner)
    gelu_value = 0.5 * pre_act * (1.0 + tanh_v)
    gelu_slope = 0.5 * (1.0 + tanh_v) + 0.5 * pre_act * (1.0 - tanh_v * tanh_v) * GELU_C * (
        1.0 + 3.0 * GELU_K * pre_act * pre_act
    )
    return (gelu_value, gelu_slope)


def dot(left, right):
    return jnp.dot(left, right, preferred_element_type=F32)


def lead_dot(left, right):
    return lax.dot_general(left, right, (((0,), (0,)), ((), ())), preferred_element_type=F32)


def as_row(ref, first):
    return jnp.concatenate([ref[first + j : first + j + 1, :] for j in range(ROWS)], axis=1)


def kernel(
    tok_h, router_h, win_h, wout_h, cot_h,
    mixed_ref, gtok_ref, grout_ref,
    tok, cot, win, wout, tok_t, cot_t, win_t, wout_t, key_own, own, keys, keys_f, key_in,
    ex_s, comb_s, combb_s, stat, part, gpart, stat1, land1, gland1, pack, gpack, land2, gland2,
    packed, rows_s, stat_all, sg_all, sg_f, outs, back, land3, coef,
    load_sem, send_sem, recv_sem,
):
    me = lax.axis_index("seq")
    group, place = me // PLACES, lax.rem(me, PLACES)

    loads = [
        pltpu.make_async_copy(src, dst, load_sem.at[i])
        for i, (src, dst) in enumerate(
            ((router_h, key_own), (tok_h, tok), (cot_h, cot), (win_h.at[0], win), (wout_h.at[0], wout))
        )
    ]
    for load in loads:
        load.start()

    side, along = group // 4, lax.rem(group, 4)
    far_groups = [
        lax.rem(side + 1 - c // 4, 2) * 4 + lax.rem(along + FAR[c % 4], 4) for c in range(8)
    ]
    far_places = [lax.rem(place + k, PLACES) for k in (4, 3, 5, 2, 6, 1, 7)]

    def everyone(act):
        def some(i, carry):
            step = (i + 1) // 2
            p = lax.rem(place + 4 + step * (1 - 2 * lax.rem(i, 2)), PLACES)
            for g in far_groups:
                act(g * PLACES + p)
            return carry

        lax.fori_loop(0, 7, some, 0)
        for g in far_groups[:7]:
            act(g * PLACES + place)

    barrier = pltpu.get_barrier_semaphore()
    everyone(
        lambda p: pl.semaphore_signal(barrier, inc=1, device_id={"seq": p}, device_id_type=MESH)
    )

    def put(stage, src, dst, peer):
        pltpu.make_async_remote_copy(
            src_ref=src, dst_ref=dst,
            send_sem=send_sem.at[stage], recv_sem=recv_sem.at[stage],
            device_id={"seq": peer}, device_id_type=MESH,
        ).start()

    def landed(stage, others):
        pltpu.make_async_copy(others, others, recv_sem.at[stage]).wait()

    def sent(stage, others):
        pltpu.make_async_copy(others, others, send_sem.at[stage]).wait()

    def halves(ref, value):
        for g in range(GROUPS):
            rows = value[8 * g : 8 * g + 8, :]
            ref[g] = jnp.concatenate([rows[:, :HALF], rows[:, HALF:]], axis=0).astype(BF16)

    def lay(ref, value, stride):
        for j in range(ROWS):
            row, column = 8 * (j // 4), 128 * (j % 4)
            ref[pl.ds(j, 8, stride=stride), :] = value[row : row + 8, column : column + 128]

    def eight(first):
        return pl.ds(pl.multiple_of(first * 8, 8), 8)

    def strip(first):
        return pl.ds(pl.multiple_of(first * PACK, 8), 9)

    loads[0].wait()
    key_row = key_own[...].astype(F32)
    for j in range(ROWS):
        own[j : j + 1, :] = key_row[:, 128 * j : 128 * (j + 1)]
    keys[me] = own[...].astype(BF16)
    loads[1].wait()
    tok_t[...] = tok[...].T
    loads[2].wait()
    cot_t[...] = cot[...].T
    pl.semaphore_wait(barrier, SLOTS - 1)
    everyone(lambda p: put(0, keys.at[me], keys.at[me], p))
    loads[3].wait()
    win_t[...] = win[...].T
    loads[4].wait()
    wout_t[...] = wout[...].T
    landed(0, keys.at[pl.ds(0, SLOTS - 1)])
    keys_f[...] = keys[...].astype(F32).reshape(SLOTS * ROWS, 128)
    for j in range(ROWS):
        key_in[SLOTS:, 128 * j : 128 * (j + 1)] = keys_f[pl.ds(j, SLOTS, stride=8), :].astype(BF16)

    logit_t = dot(key_in[SLOTS:, :], tok_t[...])
    peak = jnp.max(logit_t, axis=1, keepdims=True)
    ex = jnp.exp(logit_t - peak)
    ex_s[...] = ex
    ex_b = ex.astype(BF16)
    total = jnp.sum(ex, axis=1, keepdims=True)
    total_b = jnp.sum(ex_b.astype(F32), axis=1, keepdims=True)
    lane = lax.broadcasted_iota(jnp.int32, (SLOTS, 128), 1)
    stat[...] = jnp.where(lane == 0, peak, jnp.where(lane == 1, total, total_b))
    for g in far_groups[:7]:
        put(1, stat.at[eight(g)], stat1.at[group], g * PLACES + place)
    stat1[group] = stat[eight(group), :]
    halves(part, dot(ex_b, tok[...]))
    for g in far_groups[:7]:
        put(2, part.at[g], land1.at[group], g * PLACES + place)
    land1[group] = part[group]

    row_peak = jnp.max(logit_t, axis=0, keepdims=True)
    row_ex = jnp.exp(logit_t - row_peak)
    comb = row_ex / jnp.sum(row_ex, axis=0, keepdims=True)
    comb_s[...] = comb
    combb_s[...] = comb.astype(BF16)
    halves(gpart, dot(combb_s[...], cot[...]))
    for g in far_groups[:7]:
        put(3, gpart.at[g], gland1.at[group], g * PLACES + place)
    gland1[group] = gpart[group]

    landed(1, stat1.at[pl.ds(0, 7)])
    peaks = stat1[:, :, 0:1]
    high = jnp.max(peaks, axis=0, keepdims=True)
    scale = jnp.exp(peaks - high)
    stat_sum = jnp.sum(stat1[...] * scale, axis=0)
    lane = lax.broadcasted_iota(jnp.int32, (8, 128), 1)
    pack[pl.ds(ROWS, 8, stride=PACK), :] = jnp.where(lane == 0, high[0], stat_sum)
    landed(2, land1.at[pl.ds(0, 7)])
    twice = jnp.concatenate([scale, scale], axis=1)
    lay(pack, jnp.sum(land1[...].astype(F32) * twice, axis=0), PACK)
    for p in far_places:
        put(4, pack.at[strip(p)], land2.at[place, pl.ds(0, 9)], group * PLACES + p)
    land2[place, :9] = pack[strip(place), :]
    landed(3, gland1.at[pl.ds(0, 7)])
    lay(gpack, jnp.sum(gland1[...].astype(F32), axis=0), ROWS)
    for p in far_places:
        put(5, gpack.at[eight(p)], gland2.at[place], group * PLACES + p)
    gland2[place] = gpack[eight(place), :]

    landed(4, land2.at[pl.ds(0, 7), pl.ds(0, 9)])
    peaks = land2[:, ROWS : ROWS + 1, 0:1]
    high = jnp.max(peaks, axis=0, keepdims=True)
    scale = jnp.exp(peaks - high)
    stat_sum = jnp.sum(land2[:, ROWS : ROWS + 1, :] * scale, axis=0)
    packed[:ROWS, :] = jnp.sum(land2[:, :ROWS, :] * scale, axis=0) / stat_sum[:, 2:3]
    slot_row = as_row(packed, 0).astype(BF16)
    gelu_value, gelu_slope = gelu_parts(dot(slot_row, win[...]))
    slot_out = dot(gelu_value.astype(BF16), wout[...])
    for j in range(ROWS):
        rows_s[j : j + 1, :] = slot_out[:, 128 * j : 128 * (j + 1)]

    landed(5, gland2.at[pl.ds(0, 7)])
    packed[ROWS:, :] = jnp.sum(gland2[...], axis=0)
    gout_row = as_row(packed, ROWS).astype(BF16)
    grad_pre = (dot(gout_row, wout_t[...]) * gelu_slope).astype(BF16)
    grad_in = dot(grad_pre, win_t[...]).astype(BF16).astype(F32)
    for j in range(ROWS):
        rows_s[ROWS + j : ROWS + j + 1, :] = grad_in[:, 128 * j : 128 * (j + 1)]
    sg_all[me] = rows_s[...].astype(BF16)
    disp_inner = jnp.sum(packed[:ROWS, :] * rows_s[ROWS:, :])
    lane = lax.broadcasted_iota(jnp.int32, (1, 128), 1)
    stat_all[me] = jnp.where(
        lane == 0, high[0], jnp.where(lane == 1, stat_sum[:, 1:2], disp_inner)
    )
    for p in far_places:
        put(6, stat_all.at[me], stat_all.at[me], group * PLACES + p)
    everyone(lambda p: put(7, sg_all.at[me], sg_all.at[me], p))
    landed(6, stat_all.at[pl.ds(0, 7)])
    mates = eight(group)
    for g in far_groups[:7]:
        put(8, stat_all.at[mates], stat_all.at[mates], g * PLACES + place)

    landed(7, sg_all.at[pl.ds(0, SLOTS - 1)])
    sg_f[...] = sg_all[...].astype(F32).reshape(SLOTS * PACK, 128)
    for j in range(ROWS):
        columns = slice(128 * j, 128 * (j + 1))
        outs[:, columns] = sg_f[pl.ds(j, SLOTS, stride=PACK), :].astype(BF16)
        key_in[:SLOTS, columns] = sg_f[pl.ds(ROWS + j, SLOTS, stride=PACK), :].astype(BF16)
    grad_comb = dot(outs[...], cot_t[...])
    comb = comb_s[...]
    comb_inner = jnp.sum(comb * grad_comb, axis=0, keepdims=True)
    logit_grad = comb * (grad_comb - comb_inner)
    grad_disp = dot(key_in[:SLOTS, :], tok_t[...])
    landed(8, stat_all.at[pl.ds(0, 56)])
    stats = stat_all[...].reshape(SLOTS, 128)
    dispatch = ex_s[...] * (jnp.exp(stat[:, 0:1] - stats[:, 0:1]) / stats[:, 1:2])
    logit_grad = logit_grad + dispatch * (grad_disp - stats[:, 2:3])
    coef[:SLOTS, :] = dispatch.astype(BF16)
    coef[SLOTS:, :] = logit_grad.astype(BF16)
    key_grad = dot(coef[SLOTS:, :], tok[...])
    for j in range(ROWS):
        back[pl.ds(j, SLOTS, stride=8), :] = key_grad[:, 128 * j : 128 * (j + 1)]

    everyone(lambda p: put(9, back.at[eight(p)], land3.at[me], p))
    land3[me] = back[eight(me), :]
    gtok_ref[...] = lead_dot(coef[...], key_in[...]).astype(BF16)
    mixed_ref[...] = lead_dot(combb_s[...], outs[...]).astype(BF16)
    landed(9, land3.at[pl.ds(0, SLOTS - 1)])
    grout_ref[...] = jnp.sum(land3[...], axis=0)

    sent(0, keys.at[pl.ds(0, SLOTS - 1)])
    sent(1, stat1.at[pl.ds(0, 7)])
    sent(2, land1.at[pl.ds(0, 7)])
    sent(3, gland1.at[pl.ds(0, 7)])
    sent(4, land2.at[pl.ds(0, 7), pl.ds(0, 9)])
    sent(5, gland2.at[pl.ds(0, 7)])
    sent(6, stat_all.at[pl.ds(0, 7)])
    sent(7, sg_all.at[pl.ds(0, SLOTS - 1)])
    sent(8, stat_all.at[pl.ds(0, 56)])
    sent(9, land3.at[pl.ds(0, SLOTS - 1)])


def store_kernel(mixed_ref, gtok_ref, grout_ref, mixed_out, gtok_out, grout_out, row, sems):
    stores = [
        pltpu.make_async_copy(mixed_ref, mixed_out, sems.at[0]),
        pltpu.make_async_copy(gtok_ref, gtok_out, sems.at[1]),
    ]
    for store in stores:
        store.start()
    row[...] = jnp.concatenate([grout_ref[j : j + 1, :] for j in range(ROWS)], axis=1)
    last = pltpu.make_async_copy(row, grout_out, sems.at[2])
    last.start()
    for store in stores:
        store.wait()
    last.wait()


def body(tokens, router, w_in, w_out, cotangent):
    anywhere = pl.BlockSpec(memory_space=pl.ANY)
    hbm = pl.BlockSpec(memory_space=pltpu.HBM)
    vmem = pl.BlockSpec(memory_space=pltpu.VMEM)
    v = pltpu.VMEM
    mixed, grad_tokens, grad_router = pl.pallas_call(
        kernel,
        out_shape=(v((TOK, D), BF16), v((TOK, D), BF16), v((ROWS, 128), F32)),
        in_specs=[hbm] * 5,
        out_specs=[vmem, vmem, vmem],
        scratch_shapes=[
            v((TOK, D), BF16), v((TOK, D), BF16), v((D, H), BF16), v((H, D), BF16),
            v((D, TOK), BF16), v((D, TOK), BF16), v((H, D), BF16), v((D, H), BF16),
            v((1, D), BF16), v((ROWS, 128), F32), v((SLOTS, ROWS, 128), BF16),
            v((SLOTS * ROWS, 128), F32), v((2 * SLOTS, D), BF16),
            v((SLOTS, TOK), F32), v((SLOTS, TOK), F32), v((SLOTS, TOK), BF16),
            v((SLOTS, 128), F32), v((GROUPS, 16, HALF), BF16), v((GROUPS, 16, HALF), BF16),
            v((GROUPS, 8, 128), F32), v((GROUPS, 16, HALF), BF16), v((GROUPS, 16, HALF), BF16),
            v((PLACES * PACK, 128), F32), v((PLACES * ROWS, 128), F32),
            v((PLACES, PACK, 128), F32), v((PLACES, ROWS, 128), F32),
            v((2 * ROWS, 128), F32), v((2 * ROWS, 128), F32),
            v((SLOTS, 1, 128), F32), v((SLOTS, PACK, 128), BF16), v((SLOTS * PACK, 128), F32),
            v((SLOTS, D), BF16), v((SLOTS * ROWS, 128), F32), v((SLOTS, ROWS, 128), F32),
            v((2 * SLOTS, TOK), BF16),
            pltpu.SemaphoreType.DMA((5,)),
            pltpu.SemaphoreType.DMA((10,)), pltpu.SemaphoreType.DMA((10,)),
        ],
        compiler_params=pltpu.CompilerParams(
            collective_id=0, has_side_effects=True, vmem_limit_bytes=60 << 20
        ),
    )(tokens, router, w_in, w_out, cotangent)
    return pl.pallas_call(
        store_kernel,
        out_shape=(
            jax.ShapeDtypeStruct((TOK, D), BF16),
            jax.ShapeDtypeStruct((TOK, D), BF16),
            jax.ShapeDtypeStruct((1, D), F32),
        ),
        in_specs=[vmem] * 3,
        out_specs=[anywhere, anywhere, anywhere],
        scratch_shapes=[v((1, D), F32), pltpu.SemaphoreType.DMA((3,))],
        compiler_params=pltpu.CompilerParams(vmem_limit_bytes=1 << 20),
    )(mixed, grad_tokens, grad_router)


def solution(mesh):
    return jax.shard_map(
        body,
        mesh=mesh,
        in_specs=(
            P(("batch", "seq"), None),
            P("seq", None),
            P("seq", None, None),
            P("seq", None, None),
            P(("batch", "seq"), None),
        ),
        out_specs=(P(("batch", "seq"), None), P(("batch", "seq"), None), P(("batch", "seq"), None)),
        check_vma=False,
    )
```

```python
import functools

import jax
import jax.numpy as jnp
from jax import lax
from jax.experimental import pallas as pl
from jax.experimental.pallas import tpu as pltpu
from jax.sharding import PartitionSpec as P

GELU_C = 0.7978845608028654
GELU_K = 0.044715
MESH = pl.DeviceIdType.MESH
F32, BF16 = jnp.float32, jnp.bfloat16

GROUPS, PLACES = 8, 8
SLOTS = GROUPS * PLACES
TOK = 512
D = 1024
H = 2048
ROWS = D // 128
PACK = 2 * ROWS
FAR = (2, 1, 3, 0)


def gelu_parts(pre_act):
    inner = GELU_C * (pre_act + GELU_K * pre_act * pre_act * pre_act)
    tanh_v = jnp.tanh(inner)
    gelu_value = 0.5 * pre_act * (1.0 + tanh_v)
    gelu_slope = 0.5 * (1.0 + tanh_v) + 0.5 * pre_act * (1.0 - tanh_v * tanh_v) * GELU_C * (
        1.0 + 3.0 * GELU_K * pre_act * pre_act
    )
    return (gelu_value, gelu_slope)


def dot(left, right):
    return jnp.dot(left, right, preferred_element_type=F32)


def lead_dot(left, right):
    return lax.dot_general(left, right, (((0,), (0,)), ((), ())), preferred_element_type=F32)


def as_row(ref, first):
    return jnp.concatenate([ref[first + j : first + j + 1, :] for j in range(ROWS)], axis=1)


def kernel(
    tok_h, router_h, win_h, wout_h, cot_h,
    mixed_ref, gtok_ref, grout_ref,
    tok, cot, win, wout, tok_t, cot_t, win_t, wout_t, key_own, own, keys, keys_f, key_in,
    ex_s, comb_s, combb_s, stat, stat1, stat_out, stat2, part, land,
    packed, rows_s, stat_all, sg_all, sg_f, outs, back, land3, coef,
    load_sem, send_sem, recv_sem,
):
    me = lax.axis_index("seq")
    group, place = me // PLACES, lax.rem(me, PLACES)

    loads = [
        pltpu.make_async_copy(src, dst, load_sem.at[i])
        for i, (src, dst) in enumerate(
            ((router_h, key_own), (tok_h, tok), (cot_h, cot), (win_h.at[0], win), (wout_h.at[0], wout))
        )
    ]
    for load in loads:
        load.start()

    side, along = group // 4, lax.rem(group, 4)
    far_groups = [
        lax.rem(side + 1 - c // 4, 2) * 4 + lax.rem(along + FAR[c % 4], 4) for c in range(8)
    ]
    far_places = [lax.rem(place + k, PLACES) for k in (4, 3, 5, 2, 6, 1, 7)]

    def everyone(act):
        def some(i, carry):
            step = (i + 1) // 2
            p = lax.rem(place + 4 + step * (1 - 2 * lax.rem(i, 2)), PLACES)
            for g in far_groups:
                act(g * PLACES + p)
            return carry

        lax.fori_loop(0, 7, some, 0)
        for g in far_groups[:7]:
            act(g * PLACES + place)

    barrier = pltpu.get_barrier_semaphore()
    everyone(
        lambda p: pl.semaphore_signal(barrier, inc=1, device_id={"seq": p}, device_id_type=MESH)
    )

    def put(stage, src, dst, peer):
        pltpu.make_async_remote_copy(
            src_ref=src, dst_ref=dst,
            send_sem=send_sem.at[stage], recv_sem=recv_sem.at[stage],
            device_id={"seq": peer}, device_id_type=MESH,
        ).start()

    def landed(stage, others):
        pltpu.make_async_copy(others, others, recv_sem.at[stage]).wait()

    def sent(stage, others):
        pltpu.make_async_copy(others, others, send_sem.at[stage]).wait()

    def eight(first):
        return pl.ds(pl.multiple_of(first * 8, 8), 8)

    loads[0].wait()
    key_row = key_own[...].astype(F32)
    for j in range(ROWS):
        own[j : j + 1, :] = key_row[:, 128 * j : 128 * (j + 1)]
    keys[me] = own[...].astype(BF16)
    loads[1].wait()
    tok_t[...] = tok[...].T
    loads[2].wait()
    cot_t[...] = cot[...].T
    pl.semaphore_wait(barrier, SLOTS - 1)
    everyone(lambda p: put(0, keys.at[me], keys.at[me], p))
    loads[3].wait()
    win_t[...] = win[...].T
    loads[4].wait()
    wout_t[...] = wout[...].T
    landed(0, keys.at[pl.ds(0, SLOTS - 1)])
    keys_f[...] = keys[...].astype(F32).reshape(SLOTS * ROWS, 128)
    for j in range(ROWS):
        key_in[SLOTS:, 128 * j : 128 * (j + 1)] = keys_f[pl.ds(j, SLOTS, stride=8), :].astype(BF16)

    logit_t = dot(key_in[SLOTS:, :], tok_t[...])
    peak = jnp.max(logit_t, axis=1, keepdims=True)
    ex = jnp.exp(logit_t - peak)
    ex_s[...] = ex
    ex_b = ex.astype(BF16)
    total = jnp.sum(ex, axis=1, keepdims=True)
    total_b = jnp.sum(ex_b.astype(F32), axis=1, keepdims=True)
    lane = lax.broadcasted_iota(jnp.int32, (SLOTS, 128), 1)
    stat[...] = jnp.where(lane == 0, peak, jnp.where(lane == 1, total, total_b))
    for g in far_groups[:7]:
        put(1, stat.at[eight(g)], stat1.at[group], g * PLACES + place)
    stat1[group] = stat[eight(group), :]

    slot_part = dot(ex_b, tok[...])
    row_peak = jnp.max(logit_t, axis=0, keepdims=True)
    row_ex = jnp.exp(logit_t - row_peak)
    comb = row_ex / jnp.sum(row_ex, axis=0, keepdims=True)
    comb_s[...] = comb
    combb_s[...] = comb.astype(BF16)
    gout_part = dot(combb_s[...], cot[...])
    for j in range(ROWS):
        columns = slice(128 * j, 128 * (j + 1))
        sg_f[pl.ds(j, SLOTS, stride=PACK), :] = slot_part[:, columns]
        sg_f[pl.ds(ROWS + j, SLOTS, stride=PACK), :] = gout_part[:, columns]
    part[...] = sg_f[...].reshape(SLOTS, PACK, 128).astype(BF16)
    mine = place * GROUPS + group
    everyone(lambda p: put(2, part.at[p], land.at[mine], p))
    land[mine] = part[me]

    landed(1, stat1.at[pl.ds(0, 7)])
    for p in range(PLACES):
        for g in range(GROUPS):
            stat_out[p * GROUPS + g] = stat1[g, p : p + 1, :]
    for p in far_places:
        put(3, stat_out.at[eight(p)], stat2.at[eight(place)], group * PLACES + p)
    stat2[eight(place)] = stat_out[eight(place)]

    landed(3, stat2.at[pl.ds(0, 56)])
    peaks = stat2[:, :, 0:1]
    high = jnp.max(peaks, axis=0, keepdims=True)
    scale = jnp.exp(peaks - high)
    stat_sum = jnp.sum(stat2[...] * scale, axis=0)
    landed(2, land.at[pl.ds(0, SLOTS - 1)])
    sums = land[...].astype(F32)
    packed[:ROWS, :] = jnp.sum(sums[:, :ROWS, :] * scale, axis=0) / stat_sum[:, 2:3]
    packed[ROWS:, :] = jnp.sum(sums[:, ROWS:, :], axis=0)
    slot_row = as_row(packed, 0).astype(BF16)
    gelu_value, gelu_slope = gelu_parts(dot(slot_row, win[...]))
    slot_out = dot(gelu_value.astype(BF16), wout[...])
    for j in range(ROWS):
        rows_s[j : j + 1, :] = slot_out[:, 128 * j : 128 * (j + 1)]

    gout_row = as_row(packed, ROWS).astype(BF16)
    grad_pre = (dot(gout_row, wout_t[...]) * gelu_slope).astype(BF16)
    grad_in = dot(grad_pre, win_t[...]).astype(BF16).astype(F32)
    for j in range(ROWS):
        rows_s[ROWS + j : ROWS + j + 1, :] = grad_in[:, 128 * j : 128 * (j + 1)]
    sg_all[me] = rows_s[...].astype(BF16)
    disp_inner = jnp.sum(packed[:ROWS, :] * rows_s[ROWS:, :])
    lane = lax.broadcasted_iota(jnp.int32, (1, 128), 1)
    stat_all[me] = jnp.where(
        lane == 0, high[0], jnp.where(lane == 1, stat_sum[:, 1:2], disp_inner)
    )
    for p in far_places:
        put(4, stat_all.at[me], stat_all.at[me], group * PLACES + p)
    everyone(lambda p: put(5, sg_all.at[me], sg_all.at[me], p))
    landed(4, stat_all.at[pl.ds(0, 7)])
    mates = eight(group)
    for g in far_groups[:7]:
        put(6, stat_all.at[mates], stat_all.at[mates], g * PLACES + place)

    landed(5, sg_all.at[pl.ds(0, SLOTS - 1)])
    sg_f[...] = sg_all[...].astype(F32).reshape(SLOTS * PACK, 128)
    for j in range(ROWS):
        columns = slice(128 * j, 128 * (j + 1))
        outs[:, columns] = sg_f[pl.ds(j, SLOTS, stride=PACK), :].astype(BF16)
        key_in[:SLOTS, columns] = sg_f[pl.ds(ROWS + j, SLOTS, stride=PACK), :].astype(BF16)
    grad_comb = dot(outs[...], cot_t[...])
    comb = comb_s[...]
    comb_inner = jnp.sum(comb * grad_comb, axis=0, keepdims=True)
    logit_grad = comb * (grad_comb - comb_inner)
    grad_disp = dot(key_in[:SLOTS, :], tok_t[...])
    landed(6, stat_all.at[pl.ds(0, 56)])
    stats = stat_all[...].reshape(SLOTS, 128)
    dispatch = ex_s[...] * (jnp.exp(stat[:, 0:1] - stats[:, 0:1]) / stats[:, 1:2])
    logit_grad = logit_grad + dispatch * (grad_disp - stats[:, 2:3])
    coef[:SLOTS, :] = dispatch.astype(BF16)
    coef[SLOTS:, :] = logit_grad.astype(BF16)
    key_grad = dot(coef[SLOTS:, :], tok[...])
    for j in range(ROWS):
        back[pl.ds(j, SLOTS, stride=8), :] = key_grad[:, 128 * j : 128 * (j + 1)]

    everyone(lambda p: put(7, back.at[eight(p)], land3.at[me], p))
    land3[me] = back[eight(me), :]
    gtok_ref[...] = lead_dot(coef[...], key_in[...]).astype(BF16)
    mixed_ref[...] = lead_dot(combb_s[...], outs[...]).astype(BF16)
    landed(7, land3.at[pl.ds(0, SLOTS - 1)])
    grout_ref[...] = jnp.sum(land3[...], axis=0)

    sent(0, keys.at[pl.ds(0, SLOTS - 1)])
    sent(1, stat1.at[pl.ds(0, 7)])
    sent(2, land.at[pl.ds(0, SLOTS - 1)])
    sent(3, stat2.at[pl.ds(0, 56)])
    sent(4, stat_all.at[pl.ds(0, 7)])
    sent(5, sg_all.at[pl.ds(0, SLOTS - 1)])
    sent(6, stat_all.at[pl.ds(0, 56)])
    sent(7, land3.at[pl.ds(0, SLOTS - 1)])


def store_kernel(mixed_ref, gtok_ref, grout_ref, mixed_out, gtok_out, grout_out, row, sems):
    stores = [
        pltpu.make_async_copy(mixed_ref, mixed_out, sems.at[0]),
        pltpu.make_async_copy(gtok_ref, gtok_out, sems.at[1]),
    ]
    for store in stores:
        store.start()
    row[...] = jnp.concatenate([grout_ref[j : j + 1, :] for j in range(ROWS)], axis=1)
    last = pltpu.make_async_copy(row, grout_out, sems.at[2])
    last.start()
    for store in stores:
        store.wait()
    last.wait()


def body(tokens, router, w_in, w_out, cotangent):
    anywhere = pl.BlockSpec(memory_space=pl.ANY)
    hbm = pl.BlockSpec(memory_space=pltpu.HBM)
    vmem = pl.BlockSpec(memory_space=pltpu.VMEM)
    v = pltpu.VMEM
    mixed, grad_tokens, grad_router = pl.pallas_call(
        kernel,
        out_shape=(v((TOK, D), BF16), v((TOK, D), BF16), v((ROWS, 128), F32)),
        in_specs=[hbm] * 5,
        out_specs=[vmem, vmem, vmem],
        scratch_shapes=[
            v((TOK, D), BF16), v((TOK, D), BF16), v((D, H), BF16), v((H, D), BF16),
            v((D, TOK), BF16), v((D, TOK), BF16), v((H, D), BF16), v((D, H), BF16),
            v((1, D), BF16), v((ROWS, 128), F32), v((SLOTS, ROWS, 128), BF16),
            v((SLOTS * ROWS, 128), F32), v((2 * SLOTS, D), BF16),
            v((SLOTS, TOK), F32), v((SLOTS, TOK), F32), v((SLOTS, TOK), BF16),
            v((SLOTS, 128), F32), v((GROUPS, PLACES, 128), F32),
            v((SLOTS, 1, 128), F32), v((SLOTS, 1, 128), F32),
            v((SLOTS, PACK, 128), BF16), v((SLOTS, PACK, 128), BF16),
            v((2 * ROWS, 128), F32), v((2 * ROWS, 128), F32),
            v((SLOTS, 1, 128), F32), v((SLOTS, PACK, 128), BF16), v((SLOTS * PACK, 128), F32),
            v((SLOTS, D), BF16), v((SLOTS * ROWS, 128), F32), v((SLOTS, ROWS, 128), F32),
            v((2 * SLOTS, TOK), BF16),
            pltpu.SemaphoreType.DMA((5,)),
            pltpu.SemaphoreType.DMA((8,)), pltpu.SemaphoreType.DMA((8,)),
        ],
        compiler_params=pltpu.CompilerParams(
            collective_id=0, has_side_effects=True, vmem_limit_bytes=60 << 20
        ),
    )(tokens, router, w_in, w_out, cotangent)
    return pl.pallas_call(
        store_kernel,
        out_shape=(
            jax.ShapeDtypeStruct((TOK, D), BF16),
            jax.ShapeDtypeStruct((TOK, D), BF16),
            jax.ShapeDtypeStruct((1, D), F32),
        ),
        in_specs=[vmem] * 3,
        out_specs=[anywhere, anywhere, anywhere],
        scratch_shapes=[v((1, D), F32), pltpu.SemaphoreType.DMA((3,))],
        compiler_params=pltpu.CompilerParams(vmem_limit_bytes=1 << 20),
    )(mixed, grad_tokens, grad_router)


def solution(mesh):
    return jax.shard_map(
        body,
        mesh=mesh,
        in_specs=(
            P(("batch", "seq"), None),
            P("seq", None),
            P("seq", None, None),
            P("seq", None, None),
            P(("batch", "seq"), None),
        ),
        out_specs=(P(("batch", "seq"), None), P(("batch", "seq"), None), P(("batch", "seq"), None)),
        check_vma=False,
    )
```

```python
import functools

import jax
import jax.numpy as jnp
from jax import lax
from jax.experimental import pallas as pl
from jax.experimental.pallas import tpu as pltpu
from jax.sharding import PartitionSpec as P

GELU_C = 0.7978845608028654
GELU_K = 0.044715
MESH = pl.DeviceIdType.MESH
F32, BF16 = jnp.float32, jnp.bfloat16

GROUPS, PLACES = 8, 8
SLOTS = GROUPS * PLACES
TOK = 512
D = 1024
H = 2048
ROWS = D // 128
HALF = D // 2
PACK = 2 * ROWS
FAR = (2, 1, 3, 0)


def gelu_parts(pre_act):
    inner = GELU_C * (pre_act + GELU_K * pre_act * pre_act * pre_act)
    tanh_v = jnp.tanh(inner)
    gelu_value = 0.5 * pre_act * (1.0 + tanh_v)
    gelu_slope = 0.5 * (1.0 + tanh_v) + 0.5 * pre_act * (1.0 - tanh_v * tanh_v) * GELU_C * (
        1.0 + 3.0 * GELU_K * pre_act * pre_act
    )
    return (gelu_value, gelu_slope)


def dot(left, right):
    return jnp.dot(left, right, preferred_element_type=F32)


def lead_dot(left, right):
    return lax.dot_general(left, right, (((0,), (0,)), ((), ())), preferred_element_type=F32)


def as_row(ref, first):
    return jnp.concatenate([ref[first + j : first + j + 1, :] for j in range(ROWS)], axis=1)


def kernel(
    tok_h, router_h, win_h, wout_h, cot_h,
    mixed_ref, gtok_ref, grout_ref,
    tok, cot, win, wout, tok_t, cot_t, win_t, wout_t, key_own, own, keys, keys_f, key_in,
    ex_s, comb_s, combb_s, stat, part, gpart, stat1, land1, gland1, pack, gpack, land2, gland2,
    packed, rows_s, stat_all, sg_all, sg_f, outs, back, back_b, land3, coef,
    load_sem, send_sem, recv_sem,
):
    me = lax.axis_index("seq")
    group, place = me // PLACES, lax.rem(me, PLACES)

    loads = [
        pltpu.make_async_copy(src, dst, load_sem.at[i])
        for i, (src, dst) in enumerate(
            ((router_h, key_own), (tok_h, tok), (cot_h, cot), (win_h.at[0], win), (wout_h.at[0], wout))
        )
    ]
    for load in loads:
        load.start()

    side, along = group // 4, lax.rem(group, 4)
    far_groups = [
        lax.rem(side + 1 - c // 4, 2) * 4 + lax.rem(along + FAR[c % 4], 4) for c in range(8)
    ]
    far_places = [lax.rem(place + k, PLACES) for k in (4, 3, 5, 2, 6, 1, 7)]

    def everyone(act):
        def some(i, carry):
            step = (i + 1) // 2
            p = lax.rem(place + 4 + step * (1 - 2 * lax.rem(i, 2)), PLACES)
            for g in far_groups:
                act(g * PLACES + p)
            return carry

        lax.fori_loop(0, 7, some, 0)
        for g in far_groups[:7]:
            act(g * PLACES + place)

    barrier = pltpu.get_barrier_semaphore()
    everyone(
        lambda p: pl.semaphore_signal(barrier, inc=1, device_id={"seq": p}, device_id_type=MESH)
    )

    def put(stage, src, dst, peer):
        pltpu.make_async_remote_copy(
            src_ref=src, dst_ref=dst,
            send_sem=send_sem.at[stage], recv_sem=recv_sem.at[stage],
            device_id={"seq": peer}, device_id_type=MESH,
        ).start()

    def landed(stage, others):
        pltpu.make_async_copy(others, others, recv_sem.at[stage]).wait()

    def sent(stage, others):
        pltpu.make_async_copy(others, others, send_sem.at[stage]).wait()

    def halves(ref, value):
        for g in range(GROUPS):
            rows = value[8 * g : 8 * g + 8, :]
            ref[g] = jnp.concatenate([rows[:, :HALF], rows[:, HALF:]], axis=0).astype(BF16)

    def lay(ref, value, stride):
        for j in range(ROWS):
            row, column = 8 * (j // 4), 128 * (j % 4)
            ref[pl.ds(j, 8, stride=stride), :] = value[row : row + 8, column : column + 128]

    def eight(first):
        return pl.ds(pl.multiple_of(first * 8, 8), 8)

    def strip(first):
        return pl.ds(pl.multiple_of(first * PACK, 8), 9)

    loads[0].wait()
    key_row = key_own[...].astype(F32)
    for j in range(ROWS):
        own[j : j + 1, :] = key_row[:, 128 * j : 128 * (j + 1)]
    keys[me] = own[...].astype(BF16)
    loads[1].wait()
    tok_t[...] = tok[...].T
    loads[2].wait()
    cot_t[...] = cot[...].T
    pl.semaphore_wait(barrier, SLOTS - 1)
    everyone(lambda p: put(0, keys.at[me], keys.at[me], p))
    loads[3].wait()
    win_t[...] = win[...].T
    loads[4].wait()
    wout_t[...] = wout[...].T
    landed(0, keys.at[pl.ds(0, SLOTS - 1)])
    keys_f[...] = keys[...].astype(F32).reshape(SLOTS * ROWS, 128)
    for j in range(ROWS):
        key_in[SLOTS:, 128 * j : 128 * (j + 1)] = keys_f[pl.ds(j, SLOTS, stride=8), :].astype(BF16)

    logit_t = dot(key_in[SLOTS:, :], tok_t[...])
    peak = jnp.max(logit_t, axis=1, keepdims=True)
    ex = jnp.exp(logit_t - peak)
    ex_s[...] = ex
    ex_b = ex.astype(BF16)
    total = jnp.sum(ex, axis=1, keepdims=True)
    total_b = jnp.sum(ex_b.astype(F32), axis=1, keepdims=True)
    lane = lax.broadcasted_iota(jnp.int32, (SLOTS, 128), 1)
    stat[...] = jnp.where(lane == 0, peak, jnp.where(lane == 1, total, total_b))
    for g in far_groups[:7]:
        put(1, stat.at[eight(g)], stat1.at[group], g * PLACES + place)
    stat1[group] = stat[eight(group), :]
    halves(part, dot(ex_b, tok[...]))
    for g in far_groups[:7]:
        put(2, part.at[g], land1.at[group], g * PLACES + place)
    land1[group] = part[group]

    row_peak = jnp.max(logit_t, axis=0, keepdims=True)
    row_ex = jnp.exp(logit_t - row_peak)
    comb = row_ex / jnp.sum(row_ex, axis=0, keepdims=True)
    comb_s[...] = comb
    combb_s[...] = comb.astype(BF16)
    halves(gpart, dot(combb_s[...], cot[...]))
    for g in far_groups[:7]:
        put(3, gpart.at[g], gland1.at[group], g * PLACES + place)
    gland1[group] = gpart[group]

    landed(1, stat1.at[pl.ds(0, 7)])
    peaks = stat1[:, :, 0:1]
    high = jnp.max(peaks, axis=0, keepdims=True)
    scale = jnp.exp(peaks - high)
    stat_sum = jnp.sum(stat1[...] * scale, axis=0)
    lane = lax.broadcasted_iota(jnp.int32, (8, 128), 1)
    pack[pl.ds(ROWS, 8, stride=PACK), :] = jnp.where(lane == 0, high[0], stat_sum)
    landed(2, land1.at[pl.ds(0, 7)])
    twice = jnp.concatenate([scale, scale], axis=1)
    lay(pack, jnp.sum(land1[...].astype(F32) * twice, axis=0), PACK)
    for p in far_places:
        put(4, pack.at[strip(p)], land2.at[place, pl.ds(0, 9)], group * PLACES + p)
    land2[place, :9] = pack[strip(place), :]
    landed(3, gland1.at[pl.ds(0, 7)])
    lay(gpack, jnp.sum(gland1[...].astype(F32), axis=0), ROWS)
    for p in far_places:
        put(5, gpack.at[eight(p)], gland2.at[place], group * PLACES + p)
    gland2[place] = gpack[eight(place), :]

    landed(4, land2.at[pl.ds(0, 7), pl.ds(0, 9)])
    peaks = land2[:, ROWS : ROWS + 1, 0:1]
    high = jnp.max(peaks, axis=0, keepdims=True)
    scale = jnp.exp(peaks - high)
    stat_sum = jnp.sum(land2[:, ROWS : ROWS + 1, :] * scale, axis=0)
    packed[:ROWS, :] = jnp.sum(land2[:, :ROWS, :] * scale, axis=0) / stat_sum[:, 2:3]
    slot_row = as_row(packed, 0).astype(BF16)
    gelu_value, gelu_slope = gelu_parts(dot(slot_row, win[...]))
    slot_out = dot(gelu_value.astype(BF16), wout[...])
    for j in range(ROWS):
        rows_s[j : j + 1, :] = slot_out[:, 128 * j : 128 * (j + 1)]

    landed(5, gland2.at[pl.ds(0, 7)])
    packed[ROWS:, :] = jnp.sum(gland2[...], axis=0)
    gout_row = as_row(packed, ROWS).astype(BF16)
    grad_pre = (dot(gout_row, wout_t[...]) * gelu_slope).astype(BF16)
    grad_in = dot(grad_pre, win_t[...]).astype(BF16).astype(F32)
    for j in range(ROWS):
        rows_s[ROWS + j : ROWS + j + 1, :] = grad_in[:, 128 * j : 128 * (j + 1)]
    sg_all[me] = rows_s[...].astype(BF16)
    disp_inner = jnp.sum(packed[:ROWS, :] * rows_s[ROWS:, :])
    lane = lax.broadcasted_iota(jnp.int32, (1, 128), 1)
    stat_all[me] = jnp.where(
        lane == 0, high[0], jnp.where(lane == 1, stat_sum[:, 1:2], disp_inner)
    )
    for p in far_places:
        put(6, stat_all.at[me], stat_all.at[me], group * PLACES + p)
    everyone(lambda p: put(7, sg_all.at[me], sg_all.at[me], p))
    landed(6, stat_all.at[pl.ds(0, 7)])
    mates = eight(group)
    for g in far_groups[:7]:
        put(8, stat_all.at[mates], stat_all.at[mates], g * PLACES + place)

    landed(7, sg_all.at[pl.ds(0, SLOTS - 1)])
    sg_f[...] = sg_all[...].astype(F32).reshape(SLOTS * PACK, 128)
    for j in range(ROWS):
        columns = slice(128 * j, 128 * (j + 1))
        outs[:, columns] = sg_f[pl.ds(j, SLOTS, stride=PACK), :].astype(BF16)
        key_in[:SLOTS, columns] = sg_f[pl.ds(ROWS + j, SLOTS, stride=PACK), :].astype(BF16)
    grad_comb = dot(outs[...], cot_t[...])
    comb = comb_s[...]
    comb_inner = jnp.sum(comb * grad_comb, axis=0, keepdims=True)
    logit_grad = comb * (grad_comb - comb_inner)
    grad_disp = dot(key_in[:SLOTS, :], tok_t[...])
    landed(8, stat_all.at[pl.ds(0, 56)])
    stats = stat_all[...].reshape(SLOTS, 128)
    dispatch = ex_s[...] * (jnp.exp(stat[:, 0:1] - stats[:, 0:1]) / stats[:, 1:2])
    logit_grad = logit_grad + dispatch * (grad_disp - stats[:, 2:3])
    coef[:SLOTS, :] = dispatch.astype(BF16)
    coef[SLOTS:, :] = logit_grad.astype(BF16)
    key_grad = dot(coef[SLOTS:, :], tok[...])
    for j in range(ROWS):
        back[pl.ds(j, SLOTS, stride=8), :] = key_grad[:, 128 * j : 128 * (j + 1)]

    back_b[...] = back[...].reshape(SLOTS, ROWS, 128).astype(BF16)
    everyone(lambda p: put(9, back_b.at[p], land3.at[me], p))
    land3[me] = back_b[me]
    gtok_ref[...] = lead_dot(coef[...], key_in[...]).astype(BF16)
    mixed_ref[...] = lead_dot(combb_s[...], outs[...]).astype(BF16)
    landed(9, land3.at[pl.ds(0, SLOTS - 1)])
    grout_ref[...] = jnp.sum(land3[...].astype(F32), axis=0)

    sent(0, keys.at[pl.ds(0, SLOTS - 1)])
    sent(1, stat1.at[pl.ds(0, 7)])
    sent(2, land1.at[pl.ds(0, 7)])
    sent(3, gland1.at[pl.ds(0, 7)])
    sent(4, land2.at[pl.ds(0, 7), pl.ds(0, 9)])
    sent(5, gland2.at[pl.ds(0, 7)])
    sent(6, stat_all.at[pl.ds(0, 7)])
    sent(7, sg_all.at[pl.ds(0, SLOTS - 1)])
    sent(8, stat_all.at[pl.ds(0, 56)])
    sent(9, land3.at[pl.ds(0, SLOTS - 1)])


def store_kernel(mixed_ref, gtok_ref, grout_ref, mixed_out, gtok_out, grout_out, row, sems):
    stores = [
        pltpu.make_async_copy(mixed_ref, mixed_out, sems.at[0]),
        pltpu.make_async_copy(gtok_ref, gtok_out, sems.at[1]),
    ]
    for store in stores:
        store.start()
    row[...] = jnp.concatenate([grout_ref[j : j + 1, :] for j in range(ROWS)], axis=1)
    last = pltpu.make_async_copy(row, grout_out, sems.at[2])
    last.start()
    for store in stores:
        store.wait()
    last.wait()


def body(tokens, router, w_in, w_out, cotangent):
    anywhere = pl.BlockSpec(memory_space=pl.ANY)
    hbm = pl.BlockSpec(memory_space=pltpu.HBM)
    vmem = pl.BlockSpec(memory_space=pltpu.VMEM)
    v = pltpu.VMEM
    mixed, grad_tokens, grad_router = pl.pallas_call(
        kernel,
        out_shape=(v((TOK, D), BF16), v((TOK, D), BF16), v((ROWS, 128), F32)),
        in_specs=[hbm] * 5,
        out_specs=[vmem, vmem, vmem],
        scratch_shapes=[
            v((TOK, D), BF16), v((TOK, D), BF16), v((D, H), BF16), v((H, D), BF16),
            v((D, TOK), BF16), v((D, TOK), BF16), v((H, D), BF16), v((D, H), BF16),
            v((1, D), BF16), v((ROWS, 128), F32), v((SLOTS, ROWS, 128), BF16),
            v((SLOTS * ROWS, 128), F32), v((2 * SLOTS, D), BF16),
            v((SLOTS, TOK), F32), v((SLOTS, TOK), F32), v((SLOTS, TOK), BF16),
            v((SLOTS, 128), F32), v((GROUPS, 16, HALF), BF16), v((GROUPS, 16, HALF), BF16),
            v((GROUPS, 8, 128), F32), v((GROUPS, 16, HALF), BF16), v((GROUPS, 16, HALF), BF16),
            v((PLACES * PACK, 128), F32), v((PLACES * ROWS, 128), F32),
            v((PLACES, PACK, 128), F32), v((PLACES, ROWS, 128), F32),
            v((2 * ROWS, 128), F32), v((2 * ROWS, 128), F32),
            v((SLOTS, 1, 128), F32), v((SLOTS, PACK, 128), BF16), v((SLOTS * PACK, 128), F32),
            v((SLOTS, D), BF16), v((SLOTS * ROWS, 128), F32), v((SLOTS, ROWS, 128), BF16), v((SLOTS, ROWS, 128), BF16),
            v((2 * SLOTS, TOK), BF16),
            pltpu.SemaphoreType.DMA((5,)),
            pltpu.SemaphoreType.DMA((10,)), pltpu.SemaphoreType.DMA((10,)),
        ],
        compiler_params=pltpu.CompilerParams(
            collective_id=0, has_side_effects=True, vmem_limit_bytes=60 << 20
        ),
    )(tokens, router, w_in, w_out, cotangent)
    return pl.pallas_call(
        store_kernel,
        out_shape=(
            jax.ShapeDtypeStruct((TOK, D), BF16),
            jax.ShapeDtypeStruct((TOK, D), BF16),
            jax.ShapeDtypeStruct((1, D), F32),
        ),
        in_specs=[vmem] * 3,
        out_specs=[anywhere, anywhere, anywhere],
        scratch_shapes=[v((1, D), F32), pltpu.SemaphoreType.DMA((3,))],
        compiler_params=pltpu.CompilerParams(vmem_limit_bytes=1 << 20),
    )(mixed, grad_tokens, grad_router)


def solution(mesh):
    return jax.shard_map(
        body,
        mesh=mesh,
        in_specs=(
            P(("batch", "seq"), None),
            P("seq", None),
            P("seq", None, None),
            P("seq", None, None),
            P(("batch", "seq"), None),
        ),
        out_specs=(P(("batch", "seq"), None), P(("batch", "seq"), None), P(("batch", "seq"), None)),
        check_vma=False,
    )
```

```python
import functools

import jax
import jax.numpy as jnp
from jax import lax
from jax.experimental import pallas as pl
from jax.experimental.pallas import tpu as pltpu
from jax.sharding import PartitionSpec as P

GELU_C = 0.7978845608028654
GELU_K = 0.044715
MESH = pl.DeviceIdType.MESH
F32, BF16 = jnp.float32, jnp.bfloat16

GROUPS, PLACES = 8, 8
SLOTS = GROUPS * PLACES
TOK = 512
D = 1024
H = 2048
ROWS = D // 128
HALF = D // 2
PACK = 2 * ROWS
FAR = (2, 1, 3, 0)
STEPS = sorted(
    [(dy, dx, dz) for dy in range(2) for dx in range(4) for dz in range(8) if dy + dx + dz],
    key=lambda o: -(o[0] + min(o[1], 4 - o[1]) + min(o[2], 8 - o[2])),
)


def gelu_parts(pre_act):
    inner = GELU_C * (pre_act + GELU_K * pre_act * pre_act * pre_act)
    tanh_v = jnp.tanh(inner)
    gelu_value = 0.5 * pre_act * (1.0 + tanh_v)
    gelu_slope = 0.5 * (1.0 + tanh_v) + 0.5 * pre_act * (1.0 - tanh_v * tanh_v) * GELU_C * (
        1.0 + 3.0 * GELU_K * pre_act * pre_act
    )
    return (gelu_value, gelu_slope)


def dot(left, right):
    return jnp.dot(left, right, preferred_element_type=F32)


def lead_dot(left, right):
    return lax.dot_general(left, right, (((0,), (0,)), ((), ())), preferred_element_type=F32)


def as_row(ref, first):
    return jnp.concatenate([ref[first + j : first + j + 1, :] for j in range(ROWS)], axis=1)


def kernel(
    tok_h, router_h, win_h, wout_h, cot_h,
    mixed_ref, gtok_ref, grout_ref,
    tok, cot, win, wout, tok_t, cot_t, win_t, wout_t, key_own, own, keys, keys_f, key_in,
    ex_s, comb_s, combb_s, stat, part, gpart, stat1, land1, gland1, pack, gpack, land2, gland2,
    packed, rows_s, stat_all, s_all, g_all, outs, back, back_b, land3, coef,
    load_sem, send_sem, recv_sem,
):
    me = lax.axis_index("seq")
    group, place = me // PLACES, lax.rem(me, PLACES)

    loads = [
        pltpu.make_async_copy(src, dst, load_sem.at[i])
        for i, (src, dst) in enumerate(
            ((router_h, key_own), (tok_h, tok), (cot_h, cot), (win_h.at[0], win), (wout_h.at[0], wout))
        )
    ]
    for load in loads:
        load.start()

    side, along = group // 4, lax.rem(group, 4)
    far_groups = [
        lax.rem(side + 1 - c // 4, 2) * 4 + lax.rem(along + FAR[c % 4], 4) for c in range(8)
    ]
    far_places = [lax.rem(place + k, PLACES) for k in (4, 3, 5, 2, 6, 1, 7)]

    def everyone(act):
        def some(i, carry):
            step = (i + 1) // 2
            p = lax.rem(place + 4 + step * (1 - 2 * lax.rem(i, 2)), PLACES)
            for g in far_groups:
                act(g * PLACES + p)
            return carry

        lax.fori_loop(0, 7, some, 0)
        for g in far_groups[:7]:
            act(g * PLACES + place)

    sides = [lax.rem(side + k, 2) * 32 for k in range(2)]
    alongs = [lax.rem(along + k, 4) * PLACES for k in range(4)]
    places = [lax.rem(place + k, PLACES) for k in range(PLACES)]

    def by_hops(act):
        for dy, dx, dz in STEPS:
            act(sides[dy] + alongs[dx] + places[dz])

    barrier = pltpu.get_barrier_semaphore()
    everyone(
        lambda p: pl.semaphore_signal(barrier, inc=1, device_id={"seq": p}, device_id_type=MESH)
    )

    def put(stage, src, dst, peer):
        pltpu.make_async_remote_copy(
            src_ref=src, dst_ref=dst,
            send_sem=send_sem.at[stage], recv_sem=recv_sem.at[stage],
            device_id={"seq": peer}, device_id_type=MESH,
        ).start()

    def landed(stage, others):
        pltpu.make_async_copy(others, others, recv_sem.at[stage]).wait()

    def sent(stage, others):
        pltpu.make_async_copy(others, others, send_sem.at[stage]).wait()

    def halves(ref, value):
        for g in range(GROUPS):
            rows = value[8 * g : 8 * g + 8, :]
            ref[g] = jnp.concatenate([rows[:, :HALF], rows[:, HALF:]], axis=0).astype(BF16)

    def lay(ref, value, stride):
        for j in range(ROWS):
            row, column = 8 * (j // 4), 128 * (j % 4)
            ref[pl.ds(j, 8, stride=stride), :] = value[row : row + 8, column : column + 128]

    def eight(first):
        return pl.ds(pl.multiple_of(first * 8, 8), 8)

    def strip(first):
        return pl.ds(pl.multiple_of(first * PACK, 8), 9)

    loads[0].wait()
    key_row = key_own[...].astype(F32)
    for j in range(ROWS):
        own[j : j + 1, :] = key_row[:, 128 * j : 128 * (j + 1)]
    keys[me] = own[...].astype(BF16)
    loads[1].wait()
    tok_t[...] = tok[...].T
    loads[2].wait()
    cot_t[...] = cot[...].T
    pl.semaphore_wait(barrier, SLOTS - 1)
    by_hops(lambda p: put(0, keys.at[me], keys.at[me], p))
    loads[3].wait()
    win_t[...] = win[...].T
    loads[4].wait()
    wout_t[...] = wout[...].T
    landed(0, keys.at[pl.ds(0, SLOTS - 1)])
    keys_f[...] = keys[...].astype(F32).reshape(SLOTS * ROWS, 128)
    for j in range(ROWS):
        key_in[SLOTS:, 128 * j : 128 * (j + 1)] = keys_f[pl.ds(j, SLOTS, stride=8), :].astype(BF16)

    logit_t = dot(key_in[SLOTS:, :], tok_t[...])
    peak = jnp.max(logit_t, axis=1, keepdims=True)
    ex = jnp.exp(logit_t - peak)
    ex_s[...] = ex
    ex_b = ex.astype(BF16)
    total = jnp.sum(ex, axis=1, keepdims=True)
    total_b = jnp.sum(ex_b.astype(F32), axis=1, keepdims=True)
    lane = lax.broadcasted_iota(jnp.int32, (SLOTS, 128), 1)
    stat[...] = jnp.where(lane == 0, peak, jnp.where(lane == 1, total, total_b))
    for g in far_groups[:7]:
        put(1, stat.at[eight(g)], stat1.at[group], g * PLACES + place)
    stat1[group] = stat[eight(group), :]
    halves(part, dot(ex_b, tok[...]))
    for g in far_groups[:7]:
        put(2, part.at[g], land1.at[group], g * PLACES + place)
    land1[group] = part[group]

    row_peak = jnp.max(logit_t, axis=0, keepdims=True)
    row_ex = jnp.exp(logit_t - row_peak)
    comb = row_ex / jnp.sum(row_ex, axis=0, keepdims=True)
    comb_s[...] = comb
    combb_s[...] = comb.astype(BF16)
    halves(gpart, dot(combb_s[...], cot[...]))
    for g in far_groups[:7]:
        put(3, gpart.at[g], gland1.at[group], g * PLACES + place)
    gland1[group] = gpart[group]

    landed(1, stat1.at[pl.ds(0, 7)])
    peaks = stat1[:, :, 0:1]
    high = jnp.max(peaks, axis=0, keepdims=True)
    scale = jnp.exp(peaks - high)
    stat_sum = jnp.sum(stat1[...] * scale, axis=0)
    lane = lax.broadcasted_iota(jnp.int32, (8, 128), 1)
    pack[pl.ds(ROWS, 8, stride=PACK), :] = jnp.where(lane == 0, high[0], stat_sum)
    landed(2, land1.at[pl.ds(0, 7)])
    twice = jnp.concatenate([scale, scale], axis=1)
    lay(pack, jnp.sum(land1[...].astype(F32) * twice, axis=0), PACK)
    for p in far_places:
        put(4, pack.at[strip(p)], land2.at[place, pl.ds(0, 9)], group * PLACES + p)
    land2[place, :9] = pack[strip(place), :]
    landed(3, gland1.at[pl.ds(0, 7)])
    lay(gpack, jnp.sum(gland1[...].astype(F32), axis=0), ROWS)
    for p in far_places:
        put(5, gpack.at[eight(p)], gland2.at[place], group * PLACES + p)
    gland2[place] = gpack[eight(place), :]

    landed(4, land2.at[pl.ds(0, 7), pl.ds(0, 9)])
    peaks = land2[:, ROWS : ROWS + 1, 0:1]
    high = jnp.max(peaks, axis=0, keepdims=True)
    scale = jnp.exp(peaks - high)
    stat_sum = jnp.sum(land2[:, ROWS : ROWS + 1, :] * scale, axis=0)
    packed[:ROWS, :] = jnp.sum(land2[:, :ROWS, :] * scale, axis=0) / stat_sum[:, 2:3]
    slot_row = as_row(packed, 0).astype(BF16)
    gelu_value, gelu_slope = gelu_parts(dot(slot_row, win[...]))
    slot_out = dot(gelu_value.astype(BF16), wout[...])
    for j in range(ROWS):
        rows_s[j : j + 1, :] = slot_out[:, 128 * j : 128 * (j + 1)]

    s_all[me] = rows_s[:ROWS, :].astype(BF16)
    for p in far_places:
        put(10, s_all.at[me], s_all.at[me], group * PLACES + p)

    landed(5, gland2.at[pl.ds(0, 7)])
    packed[ROWS:, :] = jnp.sum(gland2[...], axis=0)
    gout_row = as_row(packed, ROWS).astype(BF16)
    grad_pre = (dot(gout_row, wout_t[...]) * gelu_slope).astype(BF16)
    grad_in = dot(grad_pre, win_t[...]).astype(BF16).astype(F32)
    for j in range(ROWS):
        rows_s[ROWS + j : ROWS + j + 1, :] = grad_in[:, 128 * j : 128 * (j + 1)]
    g_all[me] = rows_s[ROWS:, :].astype(BF16)
    disp_inner = jnp.sum(packed[:ROWS, :] * rows_s[ROWS:, :])
    lane = lax.broadcasted_iota(jnp.int32, (1, 128), 1)
    stat_all[me] = jnp.where(
        lane == 0, high[0], jnp.where(lane == 1, stat_sum[:, 1:2], disp_inner)
    )
    def both(p):
        put(6, stat_all.at[me], stat_all.at[me], p)
        put(7, g_all.at[me], g_all.at[me], p)

    by_hops(both)
    mates = eight(group)
    landed(10, s_all.at[pl.ds(0, 7)])
    for g in far_groups[:7]:
        put(11, s_all.at[mates], s_all.at[mates], g * PLACES + place)

    landed(11, s_all.at[pl.ds(0, 56)])
    keys_f[...] = s_all[...].astype(F32).reshape(SLOTS * ROWS, 128)
    for j in range(ROWS):
        outs[:, 128 * j : 128 * (j + 1)] = keys_f[pl.ds(j, SLOTS, stride=8), :].astype(BF16)
    grad_comb = dot(outs[...], cot_t[...])
    comb = comb_s[...]
    comb_inner = jnp.sum(comb * grad_comb, axis=0, keepdims=True)
    logit_grad = comb * (grad_comb - comb_inner)
    landed(6, stat_all.at[pl.ds(0, SLOTS - 1)])
    landed(7, g_all.at[pl.ds(0, SLOTS - 1)])
    keys_f[...] = g_all[...].astype(F32).reshape(SLOTS * ROWS, 128)
    for j in range(ROWS):
        key_in[:SLOTS, 128 * j : 128 * (j + 1)] = keys_f[pl.ds(j, SLOTS, stride=8), :].astype(BF16)
    grad_disp = dot(key_in[:SLOTS, :], tok_t[...])
    stats = stat_all[...].reshape(SLOTS, 128)
    dispatch = ex_s[...] * (jnp.exp(stat[:, 0:1] - stats[:, 0:1]) / stats[:, 1:2])
    logit_grad = logit_grad + dispatch * (grad_disp - stats[:, 2:3])
    coef[:SLOTS, :] = dispatch.astype(BF16)
    coef[SLOTS:, :] = logit_grad.astype(BF16)
    key_grad = dot(coef[SLOTS:, :], tok[...])
    for j in range(ROWS):
        back[pl.ds(j, SLOTS, stride=8), :] = key_grad[:, 128 * j : 128 * (j + 1)]

    back_b[...] = back[...].reshape(SLOTS, ROWS, 128).astype(BF16)
    by_hops(lambda p: put(9, back_b.at[p], land3.at[me], p))
    land3[me] = back_b[me]
    gtok_ref[...] = lead_dot(coef[...], key_in[...]).astype(BF16)
    mixed_ref[...] = lead_dot(combb_s[...], outs[...]).astype(BF16)
    landed(9, land3.at[pl.ds(0, SLOTS - 1)])
    grout_ref[...] = jnp.sum(land3[...].astype(F32), axis=0)

    sent(0, keys.at[pl.ds(0, SLOTS - 1)])
    sent(1, stat1.at[pl.ds(0, 7)])
    sent(2, land1.at[pl.ds(0, 7)])
    sent(3, gland1.at[pl.ds(0, 7)])
    sent(4, land2.at[pl.ds(0, 7), pl.ds(0, 9)])
    sent(5, gland2.at[pl.ds(0, 7)])
    sent(6, stat_all.at[pl.ds(0, SLOTS - 1)])
    sent(7, g_all.at[pl.ds(0, SLOTS - 1)])
    sent(9, land3.at[pl.ds(0, SLOTS - 1)])
    sent(10, s_all.at[pl.ds(0, 7)])
    sent(11, s_all.at[pl.ds(0, 56)])


def store_kernel(mixed_ref, gtok_ref, grout_ref, mixed_out, gtok_out, grout_out, row, sems):
    stores = [
        pltpu.make_async_copy(mixed_ref, mixed_out, sems.at[0]),
        pltpu.make_async_copy(gtok_ref, gtok_out, sems.at[1]),
    ]
    for store in stores:
        store.start()
    row[...] = jnp.concatenate([grout_ref[j : j + 1, :] for j in range(ROWS)], axis=1)
    last = pltpu.make_async_copy(row, grout_out, sems.at[2])
    last.start()
    for store in stores:
        store.wait()
    last.wait()


def body(tokens, router, w_in, w_out, cotangent):
    anywhere = pl.BlockSpec(memory_space=pl.ANY)
    hbm = pl.BlockSpec(memory_space=pltpu.HBM)
    vmem = pl.BlockSpec(memory_space=pltpu.VMEM)
    v = pltpu.VMEM
    mixed, grad_tokens, grad_router = pl.pallas_call(
        kernel,
        out_shape=(v((TOK, D), BF16), v((TOK, D), BF16), v((ROWS, 128), F32)),
        in_specs=[hbm] * 5,
        out_specs=[vmem, vmem, vmem],
        scratch_shapes=[
            v((TOK, D), BF16), v((TOK, D), BF16), v((D, H), BF16), v((H, D), BF16),
            v((D, TOK), BF16), v((D, TOK), BF16), v((H, D), BF16), v((D, H), BF16),
            v((1, D), BF16), v((ROWS, 128), F32), v((SLOTS, ROWS, 128), BF16),
            v((SLOTS * ROWS, 128), F32), v((2 * SLOTS, D), BF16),
            v((SLOTS, TOK), F32), v((SLOTS, TOK), F32), v((SLOTS, TOK), BF16),
            v((SLOTS, 128), F32), v((GROUPS, 16, HALF), BF16), v((GROUPS, 16, HALF), BF16),
            v((GROUPS, 8, 128), F32), v((GROUPS, 16, HALF), BF16), v((GROUPS, 16, HALF), BF16),
            v((PLACES * PACK, 128), F32), v((PLACES * ROWS, 128), F32),
            v((PLACES, PACK, 128), F32), v((PLACES, ROWS, 128), F32),
            v((2 * ROWS, 128), F32), v((2 * ROWS, 128), F32),
            v((SLOTS, 1, 128), F32), v((SLOTS, ROWS, 128), BF16), v((SLOTS, ROWS, 128), BF16),
            v((SLOTS, D), BF16), v((SLOTS * ROWS, 128), F32), v((SLOTS, ROWS, 128), BF16), v((SLOTS, ROWS, 128), BF16),
            v((2 * SLOTS, TOK), BF16),
            pltpu.SemaphoreType.DMA((5,)),
            pltpu.SemaphoreType.DMA((12,)), pltpu.SemaphoreType.DMA((12,)),
        ],
        compiler_params=pltpu.CompilerParams(
            collective_id=0, has_side_effects=True, vmem_limit_bytes=60 << 20
        ),
    )(tokens, router, w_in, w_out, cotangent)
    return pl.pallas_call(
        store_kernel,
        out_shape=(
            jax.ShapeDtypeStruct((TOK, D), BF16),
            jax.ShapeDtypeStruct((TOK, D), BF16),
            jax.ShapeDtypeStruct((1, D), F32),
        ),
        in_specs=[vmem] * 3,
        out_specs=[anywhere, anywhere, anywhere],
        scratch_shapes=[v((1, D), F32), pltpu.SemaphoreType.DMA((3,))],
        compiler_params=pltpu.CompilerParams(vmem_limit_bytes=1 << 20),
    )(mixed, grad_tokens, grad_router)


def solution(mesh):
    return jax.shard_map(
        body,
        mesh=mesh,
        in_specs=(
            P(("batch", "seq"), None),
            P("seq", None),
            P("seq", None, None),
            P("seq", None, None),
            P(("batch", "seq"), None),
        ),
        out_specs=(P(("batch", "seq"), None), P(("batch", "seq"), None), P(("batch", "seq"), None)),
        check_vma=False,
    )
```
